32 devices in a mesh: ctx: 4 (over x, core), tp: 4 (over z), grp: 2 (over y).
Axes of the slice: x: 2, y: 2, z: 4, core: 2. Of those that a mesh axis runs over, the one named last changes fastest.
Arguments:
- pre_act: bfloat16 [2048, 5120], P(('ctx', 'grp')), may hold values from -6 to 6
- w_out: bfloat16 [5120, 8192], P(None, 'tp'), may hold values from -0.078125 to 0.078125
- b_out: bfloat16 [8192], P('tp'), may hold values from -3 to 3
- row_slot: int32 [2048], P(('ctx', 'grp')), may hold values from 0 to 511, as said below
- ctx_slot: int32 [4096], P(('ctx', 'grp')), may hold values from -1 to 511, as said below
- text_rows: bfloat16 [4096, 8192], P(('ctx', 'grp'), 'tp'), may hold values from -6 to 6
- cotangent: bfloat16 [4096, 8192], P(('ctx', 'grp'), 'tp'), may hold values from -6 to 6
Outputs:
- embeds: bfloat16 [4096, 8192], P(('ctx', 'grp'), 'tp')
- grad_pre: bfloat16 [2048, 5120], P(('ctx', 'grp'))
The draws below stay inside these ranges and needn't reach their ends.
Inputs may be any that keep to these rules, and one draw needn't show every extreme that they name: `row_slot`: within each aligned block of 256 rows (one encoder device) the values are distinct; value // 64 is the context shard (index along ctx+grp) that receives the row and value % 64 its slot there; in every block some shard receives exactly 64 rows. `ctx_slot`: within each aligned block of 512 positions (one context shard) the values other than -1 are distinct; a value s names the row that encoder device s // 64 (index along ctx+grp) sent in slot s % 64 to this shard; every image token is placed at exactly one position and every used slot names a sent row.
All inputs are finite; a program needn't handle non-finite values.
Results may differ from the reference program's by a relative error of at most 0.018.
Values may be sent and summed in bfloat16 or wider, within the bound.
No kernel may reach another device: no remote copies, remote signals or barrier semaphores. Data moves between devices by JAX's collectives and lax.ppermute only.
A program may use at most 64 MiB of HBM per device.

```python
import jax
import jax.numpy as jnp
from jax import lax

D = 8192
D_IN = 5120
ROWS_DEV = 256
TOK_DEV = 512
CAP = 64
IMAGES = 2048
CONTEXT = 4096
N_CTX = 4
N_TP = 4
N_GRP = 2


def routing_tables(key):
    groups = N_CTX * N_GRP
    slot_count = groups * CAP
    base = jax.random.fold_in(key, 9173)
    key_hot, key_noise, key_rows, key_places = jax.random.split(base, 4)
    hot_shard = jax.random.randint(key_hot, (groups,), 0, groups)
    random_part = jax.random.randint(key_noise, (groups, slot_count), 0, 65536)
    slot_ids = jnp.arange(slot_count, dtype=jnp.int32)
    is_hot = slot_ids[None, :] // CAP == hot_shard[:, None]
    forced = (jnp.arange(groups, dtype=jnp.int32)[:, None] == 0) & ((slot_ids[None, :] == 0) | (slot_ids[None, :] == slot_count - 1))
    scores = random_part * slot_count + slot_ids[None, :] + (is_hot | forced).astype(jnp.int32) * (65536 * slot_count)
    ranking = jnp.argsort(-scores, axis=1)
    chosen = ranking[:, :ROWS_DEV].astype(jnp.int32)
    row_noise = jax.random.randint(key_rows, (groups, ROWS_DEV), 0, 65536) * ROWS_DEV + jnp.arange(ROWS_DEV, dtype=jnp.int32)[None, :]
    shuffle = jnp.argsort(row_noise, axis=1)
    chosen = jnp.take_along_axis(chosen, shuffle, axis=1)
    row_slot = chosen.reshape(-1)
    in_use = jnp.zeros((groups, slot_count), jnp.int32).at[jnp.arange(groups, dtype=jnp.int32)[:, None], chosen].set(1)
    received = in_use.reshape(groups, groups, CAP).transpose(1, 0, 2).reshape(groups, slot_count)
    listing = jnp.argsort((1 - received) * slot_count + slot_ids[None, :], axis=1).astype(jnp.int32)
    counts = jnp.sum(received, axis=1)
    place_noise = jax.random.randint(key_places, (groups, TOK_DEV), 0, 65536) * TOK_DEV + jnp.arange(TOK_DEV, dtype=jnp.int32)[None, :]
    positions = jnp.argsort(place_noise, axis=1)[:, :slot_count]
    values = jnp.where(slot_ids[None, :] < counts[:, None], listing, -1)
    ctx_table = jnp.full((groups, TOK_DEV), -1, jnp.int32).at[jnp.arange(groups, dtype=jnp.int32)[:, None], positions].set(values)
    return (row_slot, ctx_table.reshape(-1))


def draw_row_slot(key, part):
    return routing_tables(key)[0]


def draw_ctx_slot(key, part):
    return routing_tables(key)[1]


def levels(rng, extent, shards, low, largest):
    def one(position, parts):
        heights = jax.random.uniform(jax.random.fold_in(jax.random.fold_in(rng, 6), position), (parts,), jnp.float32, low / len(shards), largest / len(shards))
        return jnp.repeat(jnp.exp(heights), extent[position] // parts).reshape((-1,) + (1,) * (len(extent) - position - 1))

    loudness = one(*shards[0])
    for cut in shards[1:]:
        loudness = loudness * one(*cut)
    return loudness


def scatter_about(stream_key, dims, scale, most, cuts=(), held_as=jnp.bfloat16):
    gain = levels(stream_key, dims, cuts, -0.22, 0.18) if cuts else 1.0
    result = jax.random.normal(stream_key, dims, jnp.float32) * scale * gain
    return jnp.minimum(jnp.maximum(result, -most), most).astype(held_as)


def setup_inputs(seed: int = 0) -> dict:
    key_list = jax.random.split(jax.random.key(seed), 8)
    return {
        "pre_act": scatter_about(key_list[0], (IMAGES, D_IN), 1.0, 6.0, ((0, 8),)),
        "w_out": scatter_about(key_list[1], (D_IN, D), D_IN ** -0.5, 0.078125, ((1, 4),)),
        "b_out": scatter_about(key_list[2], (D,), 0.5, 3.0, ((0, 4),)),
        "row_slot": draw_row_slot(jax.random.fold_in(key_list[7], 71), 0),
        "ctx_slot": draw_ctx_slot(jax.random.fold_in(key_list[7], 71), 0),
        "text_rows": scatter_about(key_list[5], (CONTEXT, D), 1.0, 6.0, ((0, 8), (1, 4))),
        "cotangent": scatter_about(key_list[6], (CONTEXT, D), 1.0, 6.0, ((0, 8), (1, 4))),
    }


def gelu_value(values):
    return 0.5 * values * (1.0 + lax.erf(values * 0.7071067811865476))


def gelu_slope(values):
    return 0.5 * (1.0 + lax.erf(values * 0.7071067811865476)) + values * jnp.exp(-0.5 * values * values) * 0.3989422804014327


def reference(pre_act, w_out, b_out, row_slot, ctx_slot, text_rows, cotangent):
    images = pre_act.shape[0]
    slot_count = 2 * ROWS_DEV
    width = D // N_TP
    pre_float = pre_act.astype(jnp.float32)
    hidden = gelu_value(pre_float).astype(jnp.bfloat16)
    merged = (jnp.dot(hidden, w_out, preferred_element_type=jnp.float32) + b_out.astype(jnp.float32)).astype(jnp.bfloat16)
    sender = jnp.arange(images, dtype=jnp.int32) // ROWS_DEV
    target = row_slot // CAP
    landing = target * slot_count + sender * CAP + row_slot % CAP
    lookup = jnp.zeros((N_CTX * N_GRP * slot_count,), jnp.int32).at[landing].set(jnp.arange(images, dtype=jnp.int32))
    shard_of = jnp.arange(ctx_slot.shape[0], dtype=jnp.int32) // TOK_DEV
    placed = ctx_slot >= 0
    row_at = lookup[jnp.where(placed, shard_of * slot_count + ctx_slot, 0)]
    embeds = jnp.where(placed[:, None], merged[row_at], text_rows)
    grad_rows = jnp.zeros((images, D), jnp.bfloat16).at[jnp.where(placed, row_at, images)].set(cotangent, mode="drop")
    summed = jnp.zeros((images, D_IN), jnp.float32)
    for group_index in range(N_TP):
        lower = group_index * width
        term = lax.dot_general(grad_rows[:, lower:lower + width], w_out[:, lower:lower + width], (((1,), (1,)), ((), ())), preferred_element_type=jnp.float32)
        rounded = lax.optimization_barrier(term.astype(jnp.bfloat16))
        summed = summed + rounded.astype(jnp.float32)
    grad_pre = (summed * gelu_slope(pre_float)).astype(jnp.bfloat16)
    return embeds, grad_pre
```

```python
import functools
import math

import jax
import jax.numpy as jnp
from jax import lax
from jax.experimental import pallas as pl
from jax.experimental.pallas import tpu as pltpu
from jax.sharding import PartitionSpec as P

BF = jnp.bfloat16
F32 = jnp.float32
I32 = jnp.int32
GROUP_AXES = ("ctx", "grp")
VMEM = pl.BlockSpec(memory_space=pltpu.VMEM)
SMEM = pl.BlockSpec(memory_space=pltpu.SMEM)
ANY = pl.BlockSpec(memory_space=pl.ANY)


def gelu_value(values):
    return 0.5 * values * (1.0 + lax.erf(values * 0.7071067811865476))


def gelu_slope(values):
    return (
        0.5 * (1.0 + lax.erf(values * 0.7071067811865476))
        + values * jnp.exp(-0.5 * values * values) * 0.3989422804014327
    )


def plain(pre_act, w_out, b_out, row_slot, ctx_slot, text_rows, cotangent):
    groups = lax.axis_size("ctx") * lax.axis_size("grp")
    slot_count = 2 * pre_act.shape[0]
    capacity = slot_count // groups
    width = w_out.shape[1]
    pre_float = pre_act.astype(F32)
    hidden = gelu_value(pre_float).astype(BF)
    merged = (jnp.dot(hidden, w_out, preferred_element_type=F32) + b_out.astype(F32)).astype(BF)
    outgoing = jnp.zeros((slot_count, width), BF).at[row_slot].set(merged)
    placed = ctx_slot >= 0
    returning = (
        jnp.zeros((slot_count, width), BF)
        .at[jnp.where(placed, ctx_slot, slot_count)]
        .set(cotangent, mode="drop")
    )

    def exchange(sent):
        blocks = sent.reshape(groups, capacity, width)
        return lax.all_to_all(
            blocks, GROUP_AXES, split_axis=0, concat_axis=0, tiled=True
        ).reshape(slot_count, width)

    arrived = exchange(outgoing)
    embeds = jnp.where(placed[:, None], arrived[jnp.where(placed, ctx_slot, 0)], text_rows)
    grad_rows = exchange(returning)[row_slot]
    partial_value = lax.dot_general(
        grad_rows, w_out, (((1,), (1,)), ((), ())), preferred_element_type=F32
    )
    summed = lax.psum(partial_value.astype(BF), "tp").astype(F32)
    grad_pre = (summed * gelu_slope(pre_float)).astype(BF)
    return embeds, grad_pre


def iota(shape, axis):
    return lax.broadcasted_iota(I32, shape, axis)


def as_column(row):
    n = row.shape[1]
    return jnp.sum(jnp.where(iota((n, n), 0) == iota((n, n), 1), row, 0), axis=1, keepdims=True)


def rank_in_block(row, shift):
    column = as_column(row)
    smaller = ((column >> shift) == (row >> shift)) & (column < row) & (column >= 0)
    return jnp.sum(smaller.astype(I32), axis=0, keepdims=True)


def arrival(row, shift, early):
    n = row.shape[1]
    rank = rank_in_block(row, shift)
    is_early = (rank < early).astype(I32)
    before = jnp.sum(
        jnp.where(iota((n, n), 0) < iota((n, n), 1), as_column(is_early), 0), axis=0, keepdims=True
    )
    index = iota((1, n), 1)
    place = jnp.where(is_early > 0, before, jnp.sum(is_early) + index - before)
    return rank, is_early, place


def call(kernel, name, out_shape, in_specs, out_specs, args, deps=(), limit=8, pins=None, **more):
    n = len(args)
    pins = pins or {}
    args = [
        pltpu.with_memory_space_constraint(arg, pins[i]) if i in pins else arg
        for i, arg in enumerate(args)
    ]
    deps = [
        pltpu.with_memory_space_constraint(dep, pltpu.HBM) if dep.size > 1 << 20 else dep
        for dep in deps
    ]

    def body(*refs):
        kernel(*refs[:n], *refs[n + len(deps) :])

    return pl.pallas_call(
        body,
        out_shape=out_shape,
        in_specs=list(in_specs) + [ANY] * len(deps),
        out_specs=out_specs,
        cost_estimate=pl.CostEstimate(flops=1000, bytes_accessed=1000, transcendentals=0),
        compiler_params=pltpu.CompilerParams(vmem_limit_bytes=limit << 20),
        name=name,
        **more,
    )(*args, *deps)


def full(shape):
    return pl.BlockSpec(shape, lambda *_: (0,) * len(shape))


def columns(rows, block):
    return pl.BlockSpec((rows, block), lambda i: (0, i))


def as_hot(mask):
    return jnp.where(mask, 1.0, 0.0).astype(BF)


def pack_context(me, slots, cotangent, low, high, shift, groups, load=None, deps=()):
    count = high - low
    tokens, width = cotangent.shape
    block = 512
    spans = [slice(start, start + block) for start in range(0, width, block)]

    def kernel(me_ref, slot_ref, rows_ref, *refs):
        here_ref, sems = refs[-2:]
        slots_copy = pltpu.make_async_copy(slot_ref, here_ref, sems.at[0])
        slots_copy.start()
        if load is None:
            outs, held_ref = refs[:groups], refs[groups]
            copy = pltpu.make_async_copy(rows_ref, held_ref, sems.at[1])
        else:
            outs, held_ref = refs[1 : 1 + groups], rows_ref
            copy = pltpu.make_async_copy(refs[0].at[load[1]], refs[1 + groups], sems.at[1])
        copy.start()
        slots_copy.wait()
        row = here_ref[...]
        rank = rank_in_block(row, shift)
        used = (row >= 0) & (rank >= low) & (rank < high)
        wire = jnp.where(used, ((row >> shift) ^ me_ref[0]) * count + rank - low, -1)
        hot = as_hot(iota((groups * count, tokens), 0) == wire)
        if load is None:
            copy.wait()
        for span in spans:
            packed = jnp.dot(hot, held_ref[:, span], preferred_element_type=F32).astype(BF)
            for k, out in enumerate(outs):
                out[:, span] = packed[k * count : (k + 1) * count]
        if load is not None:
            copy.wait()

    if load is None:
        more = ()
        held = pltpu.VMEM((tokens, width), BF)
    else:
        more = (load[0],)
        held = pltpu.VMEM((load[1].stop - load[1].start, load[0].shape[1]), BF)
    pins = {1: pltpu.HBM, 2: pltpu.HBM}
    if load is not None:
        pins = {1: pltpu.HBM, 2: pltpu.VMEM, 3: pltpu.HBM}
    *outs, held = call(
        kernel,
        "pack_context",
        [jax.ShapeDtypeStruct((count, width), BF)] * groups + [held],
        [SMEM, ANY, ANY if load is None else VMEM] + [ANY] * len(more),
        [VMEM] * (groups + 1),
        (me, slots, cotangent, *more),
        deps,
        pins=pins,
        scratch_shapes=[pltpu.VMEM((1, tokens), I32), pltpu.SemaphoreType.DMA((2,))],
    )
    return outs, held


def route(me, row_slots, ctx_slots, early, shift, groups, deps=()):
    n = row_slots.shape[1]
    tokens = ctx_slots.shape[1]
    capacity = 1 << shift
    late = capacity - early
    half = n * early // capacity
    wires = groups * capacity

    def kernel(me_ref, row_ref, ctx_ref, early_ref, all_ref, back_ref, merged_ref, place_ref):
        row = row_ref[...]
        rank, is_early, place = arrival(row, shift, early)
        piece = (row >> shift) ^ me_ref[0]
        wire = jnp.where(
            is_early > 0, piece * early + rank, groups * early + piece * late + rank - early
        )
        order = iota((n, n), 0) == place
        source = jnp.sum(jnp.where(order, wire, 0), axis=1, keepdims=True)
        early_ref[...] = as_hot(iota((half, groups * early), 1) == source[:half])
        all_ref[...] = as_hot(iota((n, wires), 1) == source)
        back_ref[...] = as_hot(iota((n, n), 1) == as_column(place))
        slot = (piece << shift) + (row & (capacity - 1))
        merged_ref[...] = as_hot(iota((wires, n), 0) == slot)
        ctx = ctx_ref[...]
        slot = (((ctx >> shift) ^ me_ref[0]) << shift) + (ctx & (capacity - 1))
        slot = as_column(jnp.where(ctx >= 0, slot, -1))
        place_ref[...] = as_hot(iota((tokens, wires), 1) == slot)

    shapes = [(half, groups * early), (n, wires), (n, n), (wires, n), (tokens, wires)]
    return call(
        kernel,
        "route",
        [jax.ShapeDtypeStruct(shape, BF) for shape in shapes],
        [SMEM, VMEM, VMEM],
        [VMEM] * len(shapes),
        (me, row_slots, ctx_slots),
        deps,
    )


def dot_columns(hot, rows_ref, out_ref, block=512):
    for start in range(0, out_ref.shape[1], block):
        span = slice(start, start + block)
        out_ref[:, span] = jnp.dot(
            hot, rows_ref[:, span], preferred_element_type=F32
        ).astype(BF)


def take_rows(hot, pieces, deps=()):
    width = pieces[0].shape[1]

    def kernel(hot_ref, *refs):
        ins, out_ref, wire_ref = refs[:-2], refs[-2], refs[-1]
        start = 0
        for piece in ins:
            wire_ref[start : start + piece.shape[0]] = piece[...]
            start += piece.shape[0]
        dot_columns(hot_ref[...], wire_ref, out_ref)

    return call(
        kernel,
        "take_rows",
        jax.ShapeDtypeStruct((hot.shape[0], width), BF),
        [VMEM] * (1 + len(pieces)),
        VMEM,
        (hot, *pieces),
        deps,
        scratch_shapes=[pltpu.VMEM((hot.shape[1], width), BF)],
    )


def back_product(rows, w_rows, span, first, last, height, deps=()):
    count = span.stop - span.start
    width = last - first

    def kernel(rows_ref, w_ref, out_ref):
        product = lax.dot_general(
            rows_ref[span],
            w_ref[first:last],
            (((1,), (1,)), ((), ())),
            preferred_element_type=F32,
        ).astype(BF)
        for i in range(count // height):
            out_ref[:, i * width : (i + 1) * width] = product[i * height : (i + 1) * height]

    return call(
        kernel,
        "back_product",
        jax.ShapeDtypeStruct((height, width * count // height), BF),
        [VMEM, VMEM],
        VMEM,
        (rows, w_rows),
        deps,
        pins={1: pltpu.VMEM},
    )


def forward_product(pre_act, w_rows, before, first, load=None, deps=()):
    rows = pre_act.shape[0]
    depth, width = w_rows.shape
    block = 512

    def kernel(pre_ref, w_ref, before_ref, *refs):
        if load is not None:
            copy = pltpu.make_async_copy(refs[0].at[load[1]], refs[3], refs[-1])
            copy.start()
            refs = refs[1:]
        out_ref, slope_ref = refs[:2]
        total = refs[-2]
        for start in range(0, depth, block):
            values = pre_ref[:, first + start : first + start + block].astype(F32)
            share = 0.5 * (1.0 + lax.erf(values * 0.7071067811865476))
            slope = share + values * jnp.exp(-0.5 * values * values) * 0.3989422804014327
            span = slice(start, start + block)
            slope_ref[:, span] = slope.astype(slope_ref.dtype)
            term = jnp.dot(
                (values * share).astype(BF), w_ref[span], preferred_element_type=F32
            )
            so_far = before_ref[...].astype(F32) if start == 0 else total[...]
            if start + block < depth:
                total[...] = so_far + term
            else:
                out_ref[...] = (so_far + term).astype(out_ref.dtype)
        if load is not None:
            copy.wait()

    more, outs, pins = (), [], {1: pltpu.VMEM}
    if load is not None:
        more, pins = (load[0],), {1: pltpu.VMEM, 3: pltpu.HBM}
        outs = [pltpu.VMEM((load[1].stop - load[1].start, load[0].shape[1]), BF)]
    return call(
        kernel,
        "forward_product",
        [
            jax.ShapeDtypeStruct((rows, width), BF if load is None else F32),
            jax.ShapeDtypeStruct((rows, depth), BF),
            *outs,
        ],
        [VMEM, VMEM, VMEM] + [ANY] * len(more),
        [VMEM] * (2 + len(outs)),
        (pre_act, w_rows, before, *more),
        deps,
        pins=pins,
        scratch_shapes=[pltpu.VMEM((rows, width), F32), pltpu.SemaphoreType.DMA],
    )


def pack_merged(hot, merged, index, capacity, deps=()):
    def kernel(hot_ref, rows_ref, out_ref):
        dot_columns(hot_ref[index * capacity : (index + 1) * capacity], rows_ref, out_ref)

    return call(
        kernel,
        "pack_merged",
        jax.ShapeDtypeStruct((capacity, merged.shape[1]), BF),
        [VMEM, VMEM],
        VMEM,
        (hot, merged),
        deps,
    )


def place_rows(slots, hot, pieces, text, deps=()):
    tokens, width = text.shape
    block = 512
    total = hot.shape[1]
    spans = [slice(start, start + block) for start in range(0, width, block)]

    def kernel(slot_ref, hot_ref, text_ref, *refs):
        ins, out_ref, wire_ref, done_ref, sems = refs[:-4], *refs[-4:]
        used = as_column((slot_ref[...] >= 0).astype(I32))
        start = 0
        for piece in ins:
            wire_ref[start : start + piece.shape[0]] = piece[...]
            start += piece.shape[0]
        copies = []
        for i, span in enumerate(spans):
            rows = jnp.dot(hot_ref[...], wire_ref[:, span], preferred_element_type=F32)
            done_ref[:, span] = jnp.where(
                used > 0, rows, text_ref[:, span].astype(F32)
            ).astype(BF)
            copies.append(
                pltpu.make_async_copy(done_ref.at[:, span], out_ref.at[:, span], sems.at[i])
            )
            copies[-1].start()
        for copy in copies:
            copy.wait()

    return call(
        kernel,
        "place_rows",
        pltpu.HBM((tokens, width), BF),
        [VMEM] * (3 + len(pieces)),
        ANY,
        (slots, hot, text, *pieces),
        deps,
        limit=12,
        scratch_shapes=[
            pltpu.VMEM((total, width), BF),
            pltpu.VMEM((tokens, width), BF),
            pltpu.SemaphoreType.DMA((len(spans),)),
        ],
    )


def add_term(own, other, deps=()):
    def kernel(a_ref, b_ref, out_ref):
        out_ref[...] = (a_ref[...].astype(F32) + b_ref[...].astype(F32)).astype(BF)

    shape = jax.ShapeDtypeStruct(own.shape, BF)
    return call(
        kernel, "add_term", shape, [VMEM, VMEM], VMEM, (own, other), deps, limit=4
    )


def add_and_choose(me, own, other, term, deps=()):
    def kernel(me_ref, a_ref, b_ref, term_ref, sum_ref, next_ref):
        total = (a_ref[...].astype(F32) + b_ref[...].astype(F32)).astype(BF)
        sum_ref[...] = total
        next_ref[...] = jnp.where(
            me_ref[1] > 0, total.astype(F32), term_ref[...].astype(F32)
        ).astype(BF)

    shape = jax.ShapeDtypeStruct(own.shape, BF)
    return call(
        kernel,
        "add_and_choose",
        (shape, shape),
        [SMEM, VMEM, VMEM, VMEM],
        (VMEM, VMEM),
        (me, own, other, term),
        deps,
        limit=4,
    )


def finish(me, hot, sums, slope, depth, so_far, first, width, deps=()):
    n = hot.shape[0]
    flat = [array for pair in sums for array in pair]
    slope, start_at = slope

    def kernel(me_ref, hot_ref, slope_ref, *refs):
        ins = refs[: len(flat)]
        out_ref, rows_ref, done_ref, sem = refs[-4:]
        start = 0
        for held, came in zip(ins[::2], ins[1::2]):
            block = jnp.where(
                me_ref[1] > 0, held[...].astype(F32), came[...].astype(F32)
            ).astype(BF)
            height = held.shape[0]
            for i in range(held.shape[1] // width):
                rows_ref[start : start + height] = block[:, i * width : (i + 1) * width]
                start += height
        total = jnp.dot(hot_ref[...], rows_ref[...], preferred_element_type=F32)
        slopes = slope_ref[:, first - start_at : first - start_at + width]
        done_ref[...] = (total * slopes.astype(F32)).astype(BF)
        copy = pltpu.make_async_copy(done_ref, out_ref.at[:, first : first + width], sem)
        copy.start()
        copy.wait()

    args = (me, hot, slope, *flat)
    in_specs = [SMEM] + [VMEM] * (2 + len(flat))
    aliases, pins = {}, {}
    if so_far is not None:
        aliases = {len(args): 0}
        pins = {len(args): pltpu.HBM}
        args += (so_far,)
        in_specs.append(ANY)
    return call(
        kernel,
        "finish",
        pltpu.HBM((n, depth), BF),
        in_specs,
        ANY,
        args,
        deps,
        pins=pins,
        scratch_shapes=[
            pltpu.VMEM((n, width), BF),
            pltpu.VMEM((n, width), BF),
            pltpu.SemaphoreType.DMA,
        ],
        input_output_aliases=aliases,
    )


def pipelined(pre_act, w_out, b_out, row_slot, ctx_slot, text_rows, cotangent):
    ctx_size, grp_size, tp_size = (lax.axis_size(name) for name in ("ctx", "grp", "tp"))
    groups = ctx_size * grp_size
    rows, depth = pre_act.shape
    width = w_out.shape[1]
    tokens = ctx_slot.shape[0]
    capacity = 2 * rows // groups
    shift = capacity.bit_length() - 1
    tp_index = lax.axis_index("tp")
    me = jnp.stack(
        [
            lax.axis_index("ctx") * grp_size + lax.axis_index("grp"),
            ((tp_index == 1) | (tp_index == 2)).astype(I32),
        ]
    )
    row_slots = row_slot.reshape(1, rows)
    ctx_slots = ctx_slot.reshape(1, tokens)

    def exchange(k, piece):
        return lax.ppermute(piece, GROUP_AXES, [(i, i ^ k) for i in range(groups)])

    def exchange_all(pieces):
        return [pieces[0]] + [exchange(k, pieces[k]) for k in range(1, groups)]

    early = capacity // 2
    early_rows = rows // 2
    first_part, second_part, every = (
        slice(0, early_rows), slice(early_rows, rows), slice(0, rows)
    )
    wide, narrow = depth // 5, depth // 10
    cut = 3 * wide
    blocks = [(first_part, c, c + wide) for c in range(0, cut, wide)]
    blocks += [(second_part, c, c + wide) for c in range(0, cut, wide)]
    blocks += [(every, c, c + narrow) for c in range(cut, depth, narrow)]
    chunks = len(blocks)

    bias = b_out.reshape(1, width)
    first_out, held = pack_context(me, ctx_slots, cotangent, 0, early, shift, groups)
    first_in = exchange_all(first_out)
    second_out, w_low = pack_context(
        me,
        ctx_slots,
        held,
        early,
        capacity,
        shift,
        groups,
        (w_out, slice(0, cut)),
        (first_out[1], bias),
    )
    second_in = exchange_all(second_out)
    hot_early, hot_all, hot_back, hot_merged, hot_place = route(
        me, row_slots, ctx_slots, early, shift, groups, (second_out[1],)
    )

    def product(j, deps=()):
        span, first, last = blocks[j]
        w_rows, start = (w_low, 0) if last <= cut else (w_high, cut)
        return back_product(grads, w_rows, span, first - start, last - start, early_rows, deps)

    grads = take_rows(hot_early, first_in)
    terms = {0: product(0)}
    terms[1] = product(1, (terms[0],))

    outer_pairs = [(0, 1), (1, 0), (2, 3), (3, 2)]
    inner_pairs = [
        (c * tp_size + t, c * tp_size + 3 - t if t in (1, 2) else (c ^ 1) * tp_size + t)
        for c in range(ctx_size)
        for t in range(tp_size)
    ]
    from_pair, from_far, halves, totals, send = {}, {}, {}, {}, {}
    outgoing, arrived = {}, {}

    def to_pair(j, value):
        from_pair[j] = lax.ppermute(value, "tp", outer_pairs)

    def sums_of(*indices):
        return [(totals[k], from_pair[k + 3]) for k in indices]

    def slope_at(column):
        return (slopes[0], 0) if column < cut else (slopes[1], cut)

    def finish_block(k, so_far, *deps):
        _, column, stop = blocks[k]
        indices = (k, k + 3) if k < 3 else (k,)
        return finish(
            me,
            hot_back,
            sums_of(*indices),
            slope_at(column),
            depth,
            so_far,
            column,
            stop - column,
            deps,
        )

    to_pair(0, terms[0])
    to_pair(1, terms[1])
    slopes = {}
    merged = None
    grad_pre = None
    sent_at = {}
    for k in range(1, groups):
        sent_at.setdefault(4 + (k - 1) * 5 // max(groups - 1, 1), []).append(groups - k)
    for j in range(chunks):
        after = []
        ahead = j + 2
        if ahead < chunks:
            previous = (send[j + 1],) if j >= 2 else (terms[ahead - 1],)
            if ahead == 3:
                grads = take_rows(hot_all, first_in + second_in, previous)
            terms[ahead] = product(ahead, previous)
            after.append(terms[ahead])
        if j == 0:
            partial, slopes[0], w_high = forward_product(
                pre_act,
                w_low,
                bias,
                0,
                (w_out, slice(cut, depth)),
                (terms[2],),
            )
            after.append(slopes[0])
        if j == 3:
            merged, slopes[1] = forward_product(
                pre_act, w_high, partial, cut, deps=(terms[ahead],)
            )
            after.append(merged)
        for k in sent_at.get(j, ()):
            outgoing[k] = pack_merged(hot_merged, merged, k, capacity, (terms[ahead],) if ahead in terms else ())
            arrived[k] = exchange(k, outgoing[k])
            after.append(outgoing[k])
        for k in sent_at.get(j - 2, ()):
            after.append(arrived[k])
        if 7 <= j:
            grad_pre = finish_block(j - 7, grad_pre)
            after.append(grad_pre)
        halves[j] = add_term(terms[j], from_pair[j], tuple(after))
        from_far[j] = lax.ppermute(halves[j], ("ctx", "tp"), inner_pairs)
        if j == 0:
            value, _ = lax.optimization_barrier((terms[2], halves[0]))
            to_pair(2, value)
        elif ahead < chunks:
            totals[j - 1], send[ahead] = add_and_choose(
                me, halves[j - 1], from_far[j - 1], terms[ahead], (halves[j],)
            )
            to_pair(ahead, send[ahead])
        else:
            totals[j - 1] = add_term(halves[j - 1], from_far[j - 1], (halves[j],))
            to_pair(ahead, totals[j - 1])
    arrived[0] = pack_merged(hot_merged, merged, 0, capacity, (totals[chunks - 2],))
    embeds = place_rows(
        ctx_slots,
        hot_place,
        [arrived[k] for k in range(groups)],
        text_rows,
        (totals[chunks - 2],),
    )
    totals[chunks - 1] = add_term(halves[chunks - 1], from_far[chunks - 1], (embeds,))
    to_pair(chunks + 2, totals[chunks - 1])
    for k in range(6, chunks):
        grad_pre = finish_block(k, grad_pre)
    return embeds, grad_pre


def shards(pre_act, w_out, b_out, row_slot, ctx_slot, text_rows, cotangent):
    groups = lax.axis_size("ctx") * lax.axis_size("grp")
    rows, depth = pre_act.shape
    width = w_out.shape[1]
    capacity = 2 * rows // groups
    power = lambda value: value & (value - 1) == 0
    fits = (
        lax.axis_size("tp") == 4
        and lax.axis_size("ctx") % 2 == 0
        and 2 <= groups <= 8
        and power(groups)
        and power(capacity)
        and capacity % 32 == 0
        and rows % 256 == 0
        and ctx_slot.shape[0] % 128 == 0
        and depth % 640 == 0
        and width % 512 == 0
    )
    plan = pipelined if fits else plain
    return plan(pre_act, w_out, b_out, row_slot, ctx_slot, text_rows, cotangent)


def solution(mesh):
    in_specs = (
        P(("ctx", "grp"), None),
        P(None, "tp"),
        P("tp"),
        P(("ctx", "grp")),
        P(("ctx", "grp")),
        P(("ctx", "grp"), "tp"),
        P(("ctx", "grp"), "tp"),
    )
    out_specs = (P(("ctx", "grp"), "tp"), P(("ctx", "grp"), None))
    return jax.shard_map(shards, mesh=mesh, in_specs=in_specs, out_specs=out_specs, check_vma=False)
```

```python
import functools
import math

import jax
import jax.numpy as jnp
from jax import lax
from jax.experimental import pallas as pl
from jax.experimental.pallas import tpu as pltpu
from jax.sharding import PartitionSpec as P

BF = jnp.bfloat16
F32 = jnp.float32
I32 = jnp.int32
GROUP_AXES = ("ctx", "grp")
VMEM = pl.BlockSpec(memory_space=pltpu.VMEM)
SMEM = pl.BlockSpec(memory_space=pltpu.SMEM)
ANY = pl.BlockSpec(memory_space=pl.ANY)
NODE = 800_000_000
TAKE = 3_200_000_000
PLACE = 6_400_000_000


def gelu_value(values):
    return 0.5 * values * (1.0 + lax.erf(values * 0.7071067811865476))


def gelu_slope(values):
    return (
        0.5 * (1.0 + lax.erf(values * 0.7071067811865476))
        + values * jnp.exp(-0.5 * values * values) * 0.3989422804014327
    )


def plain(pre_act, w_out, b_out, row_slot, ctx_slot, text_rows, cotangent):
    groups = lax.axis_size("ctx") * lax.axis_size("grp")
    slot_count = 2 * pre_act.shape[0]
    capacity = slot_count // groups
    width = w_out.shape[1]
    pre_float = pre_act.astype(F32)
    hidden = gelu_value(pre_float).astype(BF)
    merged = (jnp.dot(hidden, w_out, preferred_element_type=F32) + b_out.astype(F32)).astype(BF)
    outgoing = jnp.zeros((slot_count, width), BF).at[row_slot].set(merged)
    placed = ctx_slot >= 0
    returning = (
        jnp.zeros((slot_count, width), BF)
        .at[jnp.where(placed, ctx_slot, slot_count)]
        .set(cotangent, mode="drop")
    )

    def exchange(sent):
        blocks = sent.reshape(groups, capacity, width)
        return lax.all_to_all(
            blocks, GROUP_AXES, split_axis=0, concat_axis=0, tiled=True
        ).reshape(slot_count, width)

    arrived = exchange(outgoing)
    embeds = jnp.where(placed[:, None], arrived[jnp.where(placed, ctx_slot, 0)], text_rows)
    grad_rows = exchange(returning)[row_slot]
    partial_value = lax.dot_general(
        grad_rows, w_out, (((1,), (1,)), ((), ())), preferred_element_type=F32
    )
    summed = lax.psum(partial_value.astype(BF), "tp").astype(F32)
    grad_pre = (summed * gelu_slope(pre_float)).astype(BF)
    return embeds, grad_pre


def iota(shape, axis):
    return lax.broadcasted_iota(I32, shape, axis)


def as_column(row):
    n = row.shape[1]
    return jnp.sum(jnp.where(iota((n, n), 0) == iota((n, n), 1), row, 0), axis=1, keepdims=True)


def rank_in_block(row, shift):
    column = as_column(row)
    smaller = ((column >> shift) == (row >> shift)) & (column < row) & (column >= 0)
    return jnp.sum(smaller.astype(I32), axis=0, keepdims=True)


def arrival(row, shift, early):
    n = row.shape[1]
    rank = rank_in_block(row, shift)
    is_early = (rank < early).astype(I32)
    before = jnp.sum(
        jnp.where(iota((n, n), 0) < iota((n, n), 1), as_column(is_early), 0), axis=0, keepdims=True
    )
    index = iota((1, n), 1)
    place = jnp.where(is_early > 0, before, jnp.sum(is_early) + index - before)
    return rank, is_early, place


def call(kernel, name, out_shape, in_specs, out_specs, args, deps=(), limit=8, pins=None, flops=1000, **more):
    n = len(args)
    pins = pins or {}
    args = [
        pltpu.with_memory_space_constraint(arg, pins[i]) if i in pins else arg
        for i, arg in enumerate(args)
    ]
    deps = [
        pltpu.with_memory_space_constraint(dep, pltpu.HBM) if dep.size >= 1 << 20 else dep
        for dep in deps
    ]

    def body(*refs):
        kernel(*refs[:n], *refs[n + len(deps) :])

    return pl.pallas_call(
        body,
        out_shape=out_shape,
        in_specs=list(in_specs) + [ANY] * len(deps),
        out_specs=out_specs,
        cost_estimate=pl.CostEstimate(flops=flops, bytes_accessed=flops // 300, transcendentals=0),
        compiler_params=pltpu.CompilerParams(vmem_limit_bytes=limit << 20),
        name=name,
        **more,
    )(*args, *deps)


def full(shape):
    return pl.BlockSpec(shape, lambda *_: (0,) * len(shape))


def columns(rows, block):
    return pl.BlockSpec((rows, block), lambda i: (0, i))


def as_hot(mask):
    return jnp.where(mask, 1.0, 0.0).astype(BF)


def place_of(offset, pair):
    return ((offset & ~(2 * pair - 1)) >> 1) | (offset & (pair - 1))


def goes_to(offset, pair):
    return place_of(offset, pair) * 2 + jnp.where((offset & pair) > 0, 1, 0)


def came_from(offset, pair, groups):
    return place_of(offset, pair) + jnp.where((offset & pair) > 0, groups // 2, 0)


def pack_context(me, inner, slots, cotangent, low, high, shift, groups, pair):
    tokens, width = cotangent.shape
    count = high - low
    spans = [slice(start, start + 512) for start in range(0, width, 512)]
    parts = groups // 2
    height = 2 * count

    def kernel(me_ref, inner_ref, slot_ref, rows_ref, *refs):
        outs, held_ref, here_ref, sems = refs[:parts], *refs[parts:]
        slots_copy = pltpu.make_async_copy(slot_ref, here_ref, sems.at[0])
        copy = pltpu.make_async_copy(rows_ref, held_ref, sems.at[1])
        slots_copy.start()
        copy.start()
        slots_copy.wait()
        row = here_ref[...]
        rank = rank_in_block(row, shift)
        used = (row >= 0) & (rank >= low) & (rank < high)
        wire = goes_to((row >> shift) ^ me_ref[0], pair) * count + rank - low
        hot = as_hot(iota((groups * count, tokens), 0) == jnp.where(used, wire, -1))
        copy.wait()
        for span in spans:
            packed = jnp.dot(hot, held_ref[:, span], preferred_element_type=F32).astype(BF)
            for k, out in enumerate(outs):
                out[:, span] = packed[k * height : (k + 1) * height]

    *outs, held = call(
        kernel,
        "pack_context",
        [pltpu.VMEM((height, width), BF)] * parts + [pltpu.VMEM((tokens, width), BF)],
        [SMEM, SMEM, ANY, ANY],
        [VMEM] * (parts + 1),
        (me, inner, slots, cotangent),
        pins={2: pltpu.HBM, 3: pltpu.HBM},
        scratch_shapes=[pltpu.VMEM((1, tokens), I32), pltpu.SemaphoreType.DMA((2,))],
    )
    return outs, held


def split_rows(hot, rows, deps=()):
    height = hot.shape[0] // 2

    def kernel(hot_ref, rows_ref, stay_ref, swap_ref):
        dot_columns(hot_ref[:height], rows_ref, stay_ref)
        dot_columns(hot_ref[height:], rows_ref, swap_ref)

    return call(
        kernel,
        "split_rows",
        [pltpu.VMEM((height, rows.shape[1]), BF)] * 2,
        [VMEM, VMEM],
        [VMEM] * 2,
        (hot, rows),
        deps,
    )


def join(stay, got, index, height, deps=()):
    span = slice(index * height, (index + 1) * height)

    def kernel(stay_ref, got_ref, out_ref):
        out_ref[:height] = stay_ref[span]
        out_ref[height:] = got_ref[span]

    return call(
        kernel,
        "join",
        pltpu.VMEM((2 * height, stay.shape[1]), BF),
        [VMEM, VMEM],
        VMEM,
        (stay, got),
        deps,
    )


def relay(pieces, deps=()):
    height, width = pieces[0].shape
    half = height // 2

    def kernel(*refs):
        for i, piece in enumerate(refs[:-1]):
            refs[-1][i * half : (i + 1) * half] = piece[half:]

    return call(
        kernel,
        "relay",
        pltpu.VMEM((len(pieces) * half, width), BF),
        [VMEM] * len(pieces),
        VMEM,
        pieces,
        deps,
    )


def gelu_product(pre_ref, w_ref, slope_ref, total_ref, first, waits):
    block = 512
    for i, wait in enumerate(waits):
        span = slice(i * block, (i + 1) * block)
        values = pre_ref[:, span].astype(F32)
        share = 0.5 * (1.0 + lax.erf(values * 0.7071067811865476))
        slope = share + values * jnp.exp(-0.5 * values * values) * 0.3989422804014327
        slope_ref[:, span] = slope.astype(BF)
        wait()
        term = jnp.dot(
            (values * share).astype(BF),
            w_ref[first + i * block : first + (i + 1) * block],
            preferred_element_type=F32,
        )
        if first + i == 0:
            total_ref[...] = term
        else:
            total_ref[...] += term


def prepare(me, row_slots, ctx_slots, early, shift, groups, pair, pre_act, w_out, cut, deps=()):
    n, depth = pre_act.shape
    width = w_out.shape[1]
    tokens = ctx_slots.shape[1]
    late = (1 << shift) - early
    half = n * early >> shift
    spans = [slice(start, start + 512) for start in range(0, depth, 512)]

    def kernel(me_ref, row_hbm, ctx_hbm, pre_hbm, w_hbm, *refs):
        early_ref, late_ref, w_ref, product_ref, slope_hbm = refs[:5]
        row_ref, ctx_ref, pre_ref, slope_ref, sems = refs[5:]
        small = [
            pltpu.make_async_copy(row_hbm, row_ref, sems.at[len(spans)]),
            pltpu.make_async_copy(ctx_hbm, ctx_ref, sems.at[len(spans) + 1]),
        ]
        values_copy = pltpu.make_async_copy(
            pre_hbm.at[:, 0:cut], pre_ref, sems.at[len(spans) + 2]
        )
        slope_copy = pltpu.make_async_copy(slope_ref, slope_hbm, sems.at[len(spans) + 3])
        copies = [
            pltpu.make_async_copy(w_hbm.at[span], w_ref.at[span], sems.at[i])
            for i, span in enumerate(spans)
        ]
        for copy in [*small, values_copy, *copies]:
            copy.start()
        for copy in small:
            copy.wait()
        row = row_ref[...]
        offset = (row >> shift) ^ me_ref[0]
        rank, is_early, place = arrival(row, shift, early)
        wire = came_from(offset, pair, groups) * early + rank
        order = iota((half, n), 0) == place
        source = jnp.sum(jnp.where(order, wire, 0), axis=1, keepdims=True)
        early_ref[...] = as_hot(iota((half, groups * early), 1) == source)
        ctx = ctx_ref[...]
        offset = (ctx >> shift) ^ me_ref[0]
        rank = rank_in_block(ctx, shift)
        target = came_from(offset, pair, groups) * late + rank - early
        target = jnp.where((ctx >= 0) & (rank >= early), target, -1)
        late_ref[...] = as_hot(iota((groups * late, tokens), 0) == target)
        values_copy.wait()
        used = cut // 512
        waits = [copy.wait for copy in copies[:used]]
        gelu_product(pre_ref, w_ref, slope_ref, product_ref, 0, waits)
        slope_copy.start()
        for copy in copies[used:]:
            copy.wait()
        slope_copy.wait()

    shapes = [(half, groups * early), (groups * late, tokens), (depth, width)]
    return call(
        kernel,
        "prepare",
        [pltpu.VMEM(shape, BF) for shape in shapes]
        + [pltpu.VMEM((n, width), F32), pltpu.HBM((n, cut), BF)],
        [SMEM] + [ANY] * 4,
        [VMEM] * 4 + [ANY],
        (me, row_slots, ctx_slots, pre_act, w_out),
        deps,
        limit=10,
        pins={i: pltpu.HBM for i in range(1, 5)},
        flops=4 * n * depth * width,
        scratch_shapes=[
            pltpu.VMEM((1, n), I32),
            pltpu.VMEM((1, tokens), I32),
            pltpu.VMEM((n, cut), BF),
            pltpu.VMEM((n, cut), BF),
            pltpu.SemaphoreType.DMA((len(spans) + 4,)),
        ],
    )


def prepare_more(
    me, row_slots, ctx_slots, early, shift, groups, pair, pre_act, w_here, product, cut, deps=()
):
    n, depth = pre_act.shape
    width = w_here.shape[1]
    tokens = ctx_slots.shape[1]
    capacity = 1 << shift
    late = capacity - early
    wires = groups * capacity

    def kernel(me_ref, row_hbm, ctx_hbm, pre_hbm, w_ref, part_ref, *refs):
        all_ref, back_ref, merged_ref, place_ref, product_ref, slope_hbm = refs[:6]
        row_ref, ctx_ref, pre_ref, slope_ref, sems = refs[6:]
        small = [
            pltpu.make_async_copy(row_hbm, row_ref, sems.at[0]),
            pltpu.make_async_copy(ctx_hbm, ctx_ref, sems.at[1]),
        ]
        values_copy = pltpu.make_async_copy(pre_hbm.at[:, cut:depth], pre_ref, sems.at[2])
        slope_copy = pltpu.make_async_copy(slope_ref, slope_hbm, sems.at[3])
        for copy in [*small, values_copy]:
            copy.start()
        for copy in small:
            copy.wait()
        row = row_ref[...]
        offset = (row >> shift) ^ me_ref[0]
        rank, is_early, place = arrival(row, shift, early)
        wire = jnp.where(
            is_early > 0,
            came_from(offset, pair, groups) * early + rank,
            groups * early + goes_to(offset, pair) * late + rank - early,
        )
        order = iota((n, n), 0) == place
        source = jnp.sum(jnp.where(order, wire, 0), axis=1, keepdims=True)
        all_ref[...] = as_hot(iota((n, wires), 1) == source)
        back_ref[...] = as_hot(iota((n, n), 1) == as_column(place))
        target = (came_from(offset, pair, groups) << shift) + (row & (capacity - 1))
        merged_ref[...] = as_hot(iota((wires, n), 0) == target)
        ctx = ctx_ref[...]
        offset = (ctx >> shift) ^ me_ref[0]
        source = (goes_to(offset, pair) << shift) + (ctx & (capacity - 1))
        source = as_column(jnp.where(ctx >= 0, source, -1))
        place_ref[...] = as_hot(iota((tokens, wires), 1) == source)
        values_copy.wait()
        product_ref[...] = part_ref[...]
        waits = [lambda: None] * ((depth - cut) // 512)
        gelu_product(pre_ref, w_ref, slope_ref, product_ref, cut, waits)
        slope_copy.start()
        slope_copy.wait()

    shapes = [(n, wires), (n, n), (wires, n), (tokens, wires)]
    return call(
        kernel,
        "prepare_more",
        [pltpu.VMEM(shape, BF) for shape in shapes]
        + [pltpu.VMEM((n, width), F32), pltpu.HBM((n, depth - cut), BF)],
        [SMEM] + [ANY] * 3 + [VMEM] * 2,
        [VMEM] * 5 + [ANY],
        (me, row_slots, ctx_slots, pre_act, w_here, product),
        deps,
        pins={1: pltpu.HBM, 2: pltpu.HBM, 3: pltpu.HBM, 4: pltpu.VMEM},
        scratch_shapes=[
            pltpu.VMEM((1, n), I32),
            pltpu.VMEM((1, tokens), I32),
            pltpu.VMEM((n, depth - cut), BF),
            pltpu.VMEM((n, depth - cut), BF),
            pltpu.SemaphoreType.DMA((4,)),
        ],
    )


def dot_columns(hot, rows_ref, out_ref, block=512):
    for start in range(0, out_ref.shape[1], block):
        span = slice(start, start + block)
        out_ref[:, span] = jnp.dot(
            hot, rows_ref[:, span], preferred_element_type=F32
        ).astype(BF)


def gather(wire_ref, refs, spans):
    start = 0
    for ref, span in zip(refs, spans):
        height = span.stop - span.start
        wire_ref[start : start + height] = ref[span]
        start += height


def take_rows(hot, pieces, deps=()):
    arrays, spans = zip(*pieces)
    width = arrays[0].shape[1]

    def kernel(hot_ref, *refs):
        ins, out_ref, wire_ref = refs[:-2], refs[-2], refs[-1]
        gather(wire_ref, ins, spans)
        dot_columns(hot_ref[...], wire_ref, out_ref)

    return call(
        kernel,
        "take_rows",
        pltpu.VMEM((hot.shape[0], width), BF),
        [VMEM] * (1 + len(arrays)),
        VMEM,
        (hot, *arrays),
        deps,
        flops=TAKE,
        scratch_shapes=[pltpu.VMEM((hot.shape[1], width), BF)],
    )


def back_product(rows, w_rows, span, first, last, deps=()):
    def kernel(rows_ref, w_ref, out_ref):
        out_ref[...] = lax.dot_general(
            rows_ref[span],
            w_ref[first:last],
            (((1,), (1,)), ((), ())),
            preferred_element_type=F32,
        ).astype(BF)

    return call(
        kernel,
        "back_product",
        pltpu.VMEM((span.stop - span.start, last - first), BF),
        [VMEM, VMEM],
        VMEM,
        (rows, w_rows),
        deps,
        pins={1: pltpu.VMEM},
    )


def round_merged(product, bias, deps=()):
    def kernel(product_ref, bias_ref, out_ref):
        out_ref[...] = (product_ref[...] + bias_ref[...].astype(F32)).astype(BF)

    return call(
        kernel,
        "round_merged",
        pltpu.VMEM(product.shape, BF),
        [VMEM, VMEM],
        VMEM,
        (product, bias),
        deps,
    )


def place_rows(slots, hot, pieces, text, deps=()):
    tokens, width = text.shape
    block = 512
    total = hot.shape[1]
    arrays, parts = zip(*pieces)
    spans = [slice(start, start + block) for start in range(0, width, block)]

    def kernel(slot_ref, hot_ref, text_ref, *refs):
        ins, out_ref, wire_ref, done_ref, sems = refs[:-4], *refs[-4:]
        used = as_column((slot_ref[...] >= 0).astype(I32))
        gather(wire_ref, ins, parts)
        copies = []
        for i, span in enumerate(spans):
            rows = jnp.dot(hot_ref[...], wire_ref[:, span], preferred_element_type=F32)
            done_ref[:, span] = jnp.where(
                used > 0, rows, text_ref[:, span].astype(F32)
            ).astype(BF)
            copies.append(
                pltpu.make_async_copy(done_ref.at[:, span], out_ref.at[:, span], sems.at[i])
            )
            copies[-1].start()
        for copy in copies:
            copy.wait()

    return call(
        kernel,
        "place_rows",
        pltpu.HBM((tokens, width), BF),
        [VMEM] * (3 + len(arrays)),
        ANY,
        (slots, hot, text, *arrays),
        deps,
        limit=12,
        flops=PLACE,
        scratch_shapes=[
            pltpu.VMEM((total, width), BF),
            pltpu.VMEM((tokens, width), BF),
            pltpu.SemaphoreType.DMA((len(spans),)),
        ],
    )


def add_term(own, other, deps=(), weight=1):
    def kernel(a_ref, b_ref, out_ref):
        out_ref[...] = (a_ref[...].astype(F32) + b_ref[...].astype(F32)).astype(BF)

    shape = pltpu.VMEM(own.shape, BF)
    return call(
        kernel, "add_term", shape, [VMEM, VMEM], VMEM, (own, other), deps, limit=4, flops=weight * NODE
    )


def add_and_choose(inner, own, other, term, deps=()):
    def kernel(inner_ref, a_ref, b_ref, term_ref, sum_ref, next_ref):
        total = (a_ref[...].astype(F32) + b_ref[...].astype(F32)).astype(BF)
        sum_ref[...] = total
        next_ref[...] = jnp.where(
            inner_ref[0] > 0, total.astype(F32), term_ref[...].astype(F32)
        ).astype(BF)

    shape = pltpu.VMEM(own.shape, BF)
    return call(
        kernel,
        "add_and_choose",
        (shape, shape),
        [SMEM, VMEM, VMEM, VMEM],
        (VMEM, VMEM),
        (inner, own, other, term),
        deps,
        limit=4,
        flops=NODE,
    )


def finish(inner, hot, sums, slope, start_at, depth, so_far, first, width, deps=()):
    n = hot.shape[0]
    flat = [array for pair in sums for array in pair]

    def kernel(inner_ref, hot_ref, slope_ref, *refs):
        ins = refs[: len(flat)]
        out_ref, rows_ref, done_ref, sem = refs[-4:]
        start = 0
        for held, came in zip(ins[::2], ins[1::2]):
            block = jnp.where(
                inner_ref[0] > 0, held[...].astype(F32), came[...].astype(F32)
            ).astype(BF)
            height = held.shape[0]
            for i in range(held.shape[1] // width):
                rows_ref[start : start + height] = block[:, i * width : (i + 1) * width]
                start += height
        total = jnp.dot(hot_ref[...], rows_ref[...], preferred_element_type=F32)
        slopes = slope_ref[:, first - start_at : first - start_at + width]
        done_ref[...] = (total * slopes.astype(F32)).astype(BF)
        copy = pltpu.make_async_copy(done_ref, out_ref.at[:, first : first + width], sem)
        copy.start()
        copy.wait()

    args = (inner, hot, slope, *flat)
    in_specs = [SMEM] + [VMEM] * (2 + len(flat))
    aliases, pins = {}, {}
    if so_far is not None:
        aliases = {len(args): 0}
        pins = {len(args): pltpu.HBM}
        args += (so_far,)
        in_specs.append(ANY)
    return call(
        kernel,
        "finish",
        pltpu.HBM((n, depth), BF),
        in_specs,
        ANY,
        args,
        deps,
        pins=pins,
        scratch_shapes=[
            pltpu.VMEM((n, width), BF),
            pltpu.VMEM((n, width), BF),
            pltpu.SemaphoreType.DMA,
        ],
        input_output_aliases=aliases,
    )


def pipelined(pre_act, w_out, b_out, row_slot, ctx_slot, text_rows, cotangent):
    ctx_size, grp_size, tp_size = (lax.axis_size(name) for name in ("ctx", "grp", "tp"))
    groups = ctx_size * grp_size
    rows, depth = pre_act.shape
    width = w_out.shape[1]
    tokens = ctx_slot.shape[0]
    capacity = 2 * rows // groups
    shift = capacity.bit_length() - 1
    me = (lax.axis_index("ctx") * grp_size + lax.axis_index("grp")).reshape(1)
    tp_index = lax.axis_index("tp")
    inner = ((tp_index == 1) | (tp_index == 2)).astype(I32).reshape(1)
    row_slots = row_slot.reshape(1, rows)
    ctx_slots = ctx_slot.reshape(1, tokens)

    pair = grp_size

    def exchange(k, piece):
        return lax.ppermute(piece, GROUP_AXES, [(i, i ^ k) for i in range(groups)])

    def whole(array):
        return array, slice(0, array.shape[0])

    def exchange_pair(i, sent):
        return exchange((i // pair) * 2 * pair + i % pair, sent)

    def exchange_pairs(sent):
        return [sent[0]] + [exchange_pair(i, sent[i]) for i in range(1, len(sent))]

    def relayed(came, deps=()):
        half = came[0].shape[0] // 2
        last = exchange(pair, relay(came, deps))
        return [(array, slice(0, half)) for array in came] + [whole(last)]

    early = capacity // 2
    late = capacity - early
    early_rows = rows // 2
    per_part = 5
    size = depth // per_part
    chunks = 2 * per_part
    half = groups // 2

    bias = b_out.reshape(1, width)
    first_out, held = pack_context(
        me, inner, ctx_slots, cotangent, 0, early, shift, groups, pair
    )
    first_in = exchange_pairs(first_out)
    cut = 3 * size
    hot_early, hot_late, w_here, forward, slope_low = prepare(
        me, row_slots, ctx_slots, early, shift, groups, pair, pre_act, w_out, cut, (first_out[1],)
    )

    def exchange_in_turn(hot, sent, height, deps):
        stay, swap = split_rows(hot, sent, deps)
        got = exchange(pair, swap)
        came = [(stay, slice(0, height)), (got, slice(0, height))]
        offsets = [(i // pair) * 2 * pair + i % pair for i in range(1, half)]
        blocks = {}
        for straight in (True, False):
            after = tuple(blocks.values())
            for i, offset in enumerate(offsets, 1):
                if (offset & (offset - 1) == 0) == straight:
                    blocks[i] = exchange(offset, join(stay, got, i, height, after))
        return came + [whole(blocks[i]) for i in range(1, half)]

    def product(j, deps=()):
        span = slice(0, early_rows) if j < per_part else slice(early_rows, rows)
        first = j % per_part * size
        return back_product(grads, w_here, span, first, first + size, deps)

    first_in = relayed(first_in, (forward,))
    grads = take_rows(hot_early, first_in)
    terms = {0: product(0)}
    terms[1] = product(1, (terms[0],))
    second_in = exchange_in_turn(hot_late, held, late, (terms[1],))
    outer_pairs = [(0, 1), (1, 0), (2, 3), (3, 2)]
    inner_pairs = [
        (c * tp_size + t, c * tp_size + 3 - t if t in (1, 2) else (c ^ 1) * tp_size + t)
        for c in range(ctx_size)
        for t in range(tp_size)
    ]
    from_pair, from_far, halves, totals, send = {}, {}, {}, {}, {}

    def to_pair(j, value):
        from_pair[j] = lax.ppermute(value, "tp", outer_pairs)

    def finish_block(k, so_far, *deps):
        sums = [(totals[i], from_pair[i + 3]) for i in (k, k + per_part)]
        slope, start_at = (slope_low, 0) if k * size < cut else (slope_high, cut)
        return finish(
            inner, hot_back, sums, slope, start_at, depth, so_far, k * size, size, deps
        )

    to_pair(0, terms[0])
    to_pair(1, terms[1])
    grad_pre = None
    for j in range(chunks):
        after = []
        ahead = j + 2
        if j == 1:
            hot_all, hot_back, hot_merged, hot_place, forward, slope_high = prepare_more(
                me,
                row_slots,
                ctx_slots,
                early,
                shift,
                groups,
                pair,
                pre_act,
                w_here,
                forward,
                cut,
                (halves[j - 1] if j else terms[2],),
            )
            after.append(hot_all)
        if ahead < chunks:
            previous = (send[j + 1],) if j >= 3 else (terms[j + 1],)
            if ahead == per_part:
                grads = take_rows(hot_all, first_in + second_in, previous)
            terms[ahead] = product(ahead, previous)
            if ahead != per_part:
                after.append(terms[ahead])
        if j == 4:
            merged = round_merged(forward, bias, (halves[j - 1],))
            arrived = exchange_in_turn(hot_merged, merged, capacity, (halves[j - 1],))
        if j == chunks - 1:
            grad_pre = finish_block(0, None, halves[j - 1])
            after.append(grad_pre)
        halves[j] = add_term(terms[j], from_pair[j], tuple(after))
        from_far[j] = lax.ppermute(halves[j], ("ctx", "tp"), inner_pairs)
        if j == 0:
            value, _ = lax.optimization_barrier((terms[2], halves[0]))
            to_pair(2, value)
        elif ahead < chunks:
            for k in {1: (), 2: (1, 2)}.get(j, (j,)):
                totals[k - 1], send[k + 2] = add_and_choose(
                    inner, halves[k - 1], from_far[k - 1], terms[k + 2], (halves[j],)
                )
                to_pair(k + 2, send[k + 2])
        else:
            totals[j - 1] = add_term(halves[j - 1], from_far[j - 1], (halves[j],))
            to_pair(ahead, totals[j - 1])
    grad_pre = finish_block(1, grad_pre, totals[chunks - 2])
    totals[chunks - 1] = add_term(halves[chunks - 1], from_far[chunks - 1], (grad_pre,))
    to_pair(chunks + 2, totals[chunks - 1])
    embeds = place_rows(ctx_slots, hot_place, arrived, text_rows, (totals[chunks - 1],))
    for k in range(2, per_part):
        grad_pre = finish_block(k, grad_pre, *([embeds] if k == 3 else []))
    return embeds, grad_pre


def shards(pre_act, w_out, b_out, row_slot, ctx_slot, text_rows, cotangent):
    groups = lax.axis_size("ctx") * lax.axis_size("grp")
    rows, depth = pre_act.shape
    width = w_out.shape[1]
    capacity = 2 * rows // groups
    power = lambda value: value & (value - 1) == 0
    fits = (
        lax.axis_size("tp") == 4
        and lax.axis_size("ctx") % 2 == 0
        and 4 <= groups <= 8
        and power(groups)
        and power(capacity)
        and capacity % 32 == 0
        and rows % 256 == 0
        and ctx_slot.shape[0] % 128 == 0
        and depth % 5120 == 0
        and width % 512 == 0
    )
    plan = pipelined if fits else plain
    return plan(pre_act, w_out, b_out, row_slot, ctx_slot, text_rows, cotangent)


def solution(mesh):
    in_specs = (
        P(("ctx", "grp"), None),
        P(None, "tp"),
        P("tp"),
        P(("ctx", "grp")),
        P(("ctx", "grp")),
        P(("ctx", "grp"), "tp"),
        P(("ctx", "grp"), "tp"),
    )
    out_specs = (P(("ctx", "grp"), "tp"), P(("ctx", "grp"), None))
    return jax.shard_map(shards, mesh=mesh, in_specs=in_specs, out_specs=out_specs, check_vma=False)
```

```python
import functools
import math

import jax
import jax.numpy as jnp
from jax import lax
from jax.experimental import pallas as pl
from jax.experimental.pallas import tpu as pltpu
from jax.sharding import PartitionSpec as P

BF = jnp.bfloat16
F32 = jnp.float32
I32 = jnp.int32
GROUP_AXES = ("ctx", "grp")
VMEM = pl.BlockSpec(memory_space=pltpu.VMEM)
SMEM = pl.BlockSpec(memory_space=pltpu.SMEM)
ANY = pl.BlockSpec(memory_space=pl.ANY)
NODE = 800_000_000
TAKE = 3_200_000_000
PLACE = 6_400_000_000
FINISH = 2_000_000_000
PRODUCT = 400_000_000


def gelu_value(values):
    return 0.5 * values * (1.0 + lax.erf(values * 0.7071067811865476))


def gelu_slope(values):
    return (
        0.5 * (1.0 + lax.erf(values * 0.7071067811865476))
        + values * jnp.exp(-0.5 * values * values) * 0.3989422804014327
    )


def plain(pre_act, w_out, b_out, row_slot, ctx_slot, text_rows, cotangent):
    groups = lax.axis_size("ctx") * lax.axis_size("grp")
    slot_count = 2 * pre_act.shape[0]
    capacity = slot_count // groups
    width = w_out.shape[1]
    pre_float = pre_act.astype(F32)
    hidden = gelu_value(pre_float).astype(BF)
    merged = (jnp.dot(hidden, w_out, preferred_element_type=F32) + b_out.astype(F32)).astype(BF)
    outgoing = jnp.zeros((slot_count, width), BF).at[row_slot].set(merged)
    placed = ctx_slot >= 0
    returning = (
        jnp.zeros((slot_count, width), BF)
        .at[jnp.where(placed, ctx_slot, slot_count)]
        .set(cotangent, mode="drop")
    )

    def exchange(sent):
        blocks = sent.reshape(groups, capacity, width)
        return lax.all_to_all(
            blocks, GROUP_AXES, split_axis=0, concat_axis=0, tiled=True
        ).reshape(slot_count, width)

    arrived = exchange(outgoing)
    embeds = jnp.where(placed[:, None], arrived[jnp.where(placed, ctx_slot, 0)], text_rows)
    grad_rows = exchange(returning)[row_slot]
    partial_value = lax.dot_general(
        grad_rows, w_out, (((1,), (1,)), ((), ())), preferred_element_type=F32
    )
    summed = lax.psum(partial_value.astype(BF), "tp").astype(F32)
    grad_pre = (summed * gelu_slope(pre_float)).astype(BF)
    return embeds, grad_pre


def iota(shape, axis):
    return lax.broadcasted_iota(I32, shape, axis)


def as_column(row):
    n = row.shape[1]
    return jnp.sum(jnp.where(iota((n, n), 0) == iota((n, n), 1), row, 0), axis=1, keepdims=True)


def rank_in_block(row, shift):
    column = as_column(row)
    smaller = ((column >> shift) == (row >> shift)) & (column < row) & (column >= 0)
    return jnp.sum(smaller.astype(I32), axis=0, keepdims=True)


def arrival(row, shift, early):
    n = row.shape[1]
    rank = rank_in_block(row, shift)
    is_early = (rank < early).astype(I32)
    before = jnp.sum(
        jnp.where(iota((n, n), 0) < iota((n, n), 1), as_column(is_early), 0), axis=0, keepdims=True
    )
    index = iota((1, n), 1)
    place = jnp.where(is_early > 0, before, jnp.sum(is_early) + index - before)
    return rank, is_early, place


def call(kernel, name, out_shape, in_specs, out_specs, args, deps=(), limit=8, pins=None, flops=1000, **more):
    n = len(args)
    pins = pins or {}
    args = [
        pltpu.with_memory_space_constraint(arg, pins[i]) if i in pins else arg
        for i, arg in enumerate(args)
    ]
    deps = [
        pltpu.with_memory_space_constraint(dep, pltpu.HBM) if dep.size >= 1 << 20 else dep
        for dep in deps
    ]

    def body(*refs):
        kernel(*refs[:n], *refs[n + len(deps) :])

    return pl.pallas_call(
        body,
        out_shape=out_shape,
        in_specs=list(in_specs) + [ANY] * len(deps),
        out_specs=out_specs,
        cost_estimate=pl.CostEstimate(flops=flops, bytes_accessed=flops // 300, transcendentals=0),
        compiler_params=pltpu.CompilerParams(vmem_limit_bytes=limit << 20),
        name=name,
        **more,
    )(*args, *deps)


def full(shape):
    return pl.BlockSpec(shape, lambda *_: (0,) * len(shape))


def columns(rows, block):
    return pl.BlockSpec((rows, block), lambda i: (0, i))


def as_hot(mask):
    return jnp.where(mask, 1.0, 0.0).astype(BF)


def place_of(offset, pair):
    return ((offset & ~(2 * pair - 1)) >> 1) | (offset & (pair - 1))


def goes_to(offset, pair):
    return place_of(offset, pair) * 2 + jnp.where((offset & pair) > 0, 1, 0)


def came_from(offset, pair, groups):
    return place_of(offset, pair) + jnp.where((offset & pair) > 0, groups // 2, 0)


def pack_context(me, inner, slots, cotangent, low, high, shift, groups, pair):
    tokens, width = cotangent.shape
    count = high - low
    spans = [slice(start, start + 512) for start in range(0, width, 512)]
    parts = groups // 2
    height = 2 * count

    def kernel(me_ref, inner_ref, slot_ref, rows_ref, *refs):
        outs, held_ref, here_ref, sems = refs[:parts], *refs[parts:]
        slots_copy = pltpu.make_async_copy(slot_ref, here_ref, sems.at[0])
        copy = pltpu.make_async_copy(rows_ref, held_ref, sems.at[1])
        slots_copy.start()
        copy.start()
        slots_copy.wait()
        row = here_ref[...]
        rank = rank_in_block(row, shift)
        used = (row >= 0) & (rank >= low) & (rank < high)
        wire = goes_to((row >> shift) ^ me_ref[0], pair) * count + rank - low
        hot = as_hot(iota((groups * count, tokens), 0) == jnp.where(used, wire, -1))
        copy.wait()
        for span in spans:
            packed = jnp.dot(hot, held_ref[:, span], preferred_element_type=F32).astype(BF)
            for k, out in enumerate(outs):
                out[:, span] = packed[k * height : (k + 1) * height]

    *outs, held = call(
        kernel,
        "pack_context",
        [pltpu.VMEM((height, width), BF)] * parts + [pltpu.VMEM((tokens, width), BF)],
        [SMEM, SMEM, ANY, ANY],
        [VMEM] * (parts + 1),
        (me, inner, slots, cotangent),
        pins={2: pltpu.HBM, 3: pltpu.HBM},
        scratch_shapes=[pltpu.VMEM((1, tokens), I32), pltpu.SemaphoreType.DMA((2,))],
    )
    return outs, held


def split_rows(hot, rows, parts, deps=()):
    half, width = hot.shape[0] // 2, rows.shape[1]
    height = half // parts

    def kernel(hot_ref, rows_ref, stay_ref, *swap_refs):
        for start in range(0, width, 512):
            span = slice(start, start + 512)
            packed = jnp.dot(hot_ref[...], rows_ref[:, span], preferred_element_type=F32)
            packed = packed.astype(BF)
            stay_ref[:, span] = packed[:half]
            for i, swap_ref in enumerate(swap_refs):
                first = half + i * height
                swap_ref[:, span] = packed[first : first + height]

    stay, *swaps = call(
        kernel,
        "split_rows",
        [pltpu.VMEM((half, width), BF)] + [pltpu.VMEM((height, width), BF)] * parts,
        [VMEM, VMEM],
        [VMEM] * (1 + parts),
        (hot, rows),
        deps,
    )
    return stay, swaps


def join(stay, got, index, height, deps=()):
    span = slice(index * height, (index + 1) * height)

    def kernel(stay_ref, got_ref, out_ref):
        out_ref[:height] = stay_ref[span]
        out_ref[height:] = got_ref[...]

    return call(
        kernel,
        "join",
        pltpu.VMEM((2 * height, stay.shape[1]), BF),
        [VMEM, VMEM],
        VMEM,
        (stay, got),
        deps,
    )


def relay(pieces, deps=()):
    height, width = pieces[0].shape
    half = height // 2

    def kernel(*refs):
        for i, piece in enumerate(refs[:-1]):
            refs[-1][i * half : (i + 1) * half] = piece[half:]

    return call(
        kernel,
        "relay",
        pltpu.VMEM((len(pieces) * half, width), BF),
        [VMEM] * len(pieces),
        VMEM,
        pieces,
        deps,
    )


def prepare(me, row_slots, ctx_slots, early, shift, groups, pair, pre_act, w_out, deps=()):
    n, depth = pre_act.shape
    width = w_out.shape[1]
    tokens = ctx_slots.shape[1]
    capacity = 1 << shift
    late = capacity - early
    half = n * early // capacity
    wires = groups * capacity
    spans = [slice(start, start + 512) for start in range(0, depth, 512)]

    def kernel(me_ref, row_hbm, ctx_hbm, pre_hbm, w_hbm, *refs):
        early_ref, all_ref, back_ref, late_ref, merged_ref, place_ref = refs[:6]
        w_ref, product_ref, slope_hbm = refs[6:9]
        row_ref, ctx_ref, pre_ref, slope_ref, sems = refs[9:]
        small = [
            pltpu.make_async_copy(row_hbm, row_ref, sems.at[len(spans)]),
            pltpu.make_async_copy(ctx_hbm, ctx_ref, sems.at[len(spans) + 1]),
        ]
        values_copy = pltpu.make_async_copy(pre_hbm, pre_ref, sems.at[len(spans) + 2])
        copies = [
            pltpu.make_async_copy(w_hbm.at[span], w_ref.at[span], sems.at[i])
            for i, span in enumerate(spans)
        ]
        for copy in [*small, values_copy, *copies]:
            copy.start()
        for copy in small:
            copy.wait()
        row = row_ref[...]
        offset = (row >> shift) ^ me_ref[0]
        rank, is_early, place = arrival(row, shift, early)
        wire = jnp.where(
            is_early > 0,
            came_from(offset, pair, groups) * early + rank,
            groups * early + goes_to(offset, pair) * late + rank - early,
        )
        order = iota((n, n), 0) == place
        source = jnp.sum(jnp.where(order, wire, 0), axis=1, keepdims=True)
        early_ref[...] = as_hot(iota((half, groups * early), 1) == source[:half])
        all_ref[...] = as_hot(iota((n, wires), 1) == source)
        back_ref[...] = as_hot(iota((n, n), 1) == as_column(place))
        target = (came_from(offset, pair, groups) << shift) + (row & (capacity - 1))
        merged_ref[...] = as_hot(iota((wires, n), 0) == target)
        ctx = ctx_ref[...]
        offset = (ctx >> shift) ^ me_ref[0]
        rank = rank_in_block(ctx, shift)
        target = came_from(offset, pair, groups) * late + rank - early
        target = jnp.where((ctx >= 0) & (rank >= early), target, -1)
        late_ref[...] = as_hot(iota((groups * late, tokens), 0) == target)
        source = (goes_to(offset, pair) << shift) + (ctx & (capacity - 1))
        source = as_column(jnp.where(ctx >= 0, source, -1))
        place_ref[...] = as_hot(iota((tokens, wires), 1) == source)
        values_copy.wait()
        slope_copies = []
        for i, (copy, span) in enumerate(zip(copies, spans)):
            values = pre_ref[:, span].astype(F32)
            share = 0.5 * (1.0 + lax.erf(values * 0.7071067811865476))
            slope = share + values * jnp.exp(-0.5 * values * values) * 0.3989422804014327
            slope_ref[:, span] = slope.astype(BF)
            slope_copies.append(
                pltpu.make_async_copy(
                    slope_ref.at[:, span], slope_hbm.at[:, span], sems.at[len(spans) + 3 + i]
                )
            )
            slope_copies[-1].start()
            copy.wait()
            term = jnp.dot(
                (values * share).astype(BF), w_ref[span], preferred_element_type=F32
            )
            if i == 0:
                product_ref[...] = term
            else:
                product_ref[...] += term
        for copy in slope_copies:
            copy.wait()

    shapes = [
        (half, groups * early),
        (n, wires),
        (n, n),
        (groups * late, tokens),
        (wires, n),
        (tokens, wires),
        (depth, width),
    ]
    return call(
        kernel,
        "prepare",
        [pltpu.VMEM(shape, BF) for shape in shapes]
        + [pltpu.VMEM((n, width), F32), pltpu.HBM((n, depth), BF)],
        [SMEM] + [ANY] * 4,
        [VMEM] * 8 + [ANY],
        (me, row_slots, ctx_slots, pre_act, w_out),
        deps,
        limit=10,
        pins={i: pltpu.HBM for i in range(1, 5)},
        flops=4 * n * depth * width,
        scratch_shapes=[
            pltpu.VMEM((1, n), I32),
            pltpu.VMEM((1, tokens), I32),
            pltpu.VMEM((n, depth), BF),
            pltpu.VMEM((n, depth), BF),
            pltpu.SemaphoreType.DMA((2 * len(spans) + 3,)),
        ],
    )


def dot_columns(hot, rows_ref, out_ref, block=512):
    for start in range(0, out_ref.shape[1], block):
        span = slice(start, start + block)
        out_ref[:, span] = jnp.dot(
            hot, rows_ref[:, span], preferred_element_type=F32
        ).astype(BF)


def gather(wire_ref, refs, spans):
    start = 0
    for ref, span in zip(refs, spans):
        height = span.stop - span.start
        wire_ref[start : start + height] = ref[span]
        start += height


def take_rows(hot, pieces, deps=()):
    arrays, spans = zip(*pieces)
    width = arrays[0].shape[1]

    def kernel(hot_ref, *refs):
        ins, out_ref, wire_ref = refs[:-2], refs[-2], refs[-1]
        gather(wire_ref, ins, spans)
        dot_columns(hot_ref[...], wire_ref, out_ref)

    return call(
        kernel,
        "take_rows",
        pltpu.VMEM((hot.shape[0], width), BF),
        [VMEM] * (1 + len(arrays)),
        VMEM,
        (hot, *arrays),
        deps,
        flops=TAKE,
        scratch_shapes=[pltpu.VMEM((hot.shape[1], width), BF)],
    )


def back_product(rows, w_rows, span, first, last, deps=()):
    def kernel(rows_ref, w_ref, out_ref):
        out_ref[...] = lax.dot_general(
            rows_ref[span],
            w_ref[first:last],
            (((1,), (1,)), ((), ())),
            preferred_element_type=F32,
        ).astype(BF)

    return call(
        kernel,
        "back_product",
        pltpu.VMEM((span.stop - span.start, last - first), BF),
        [VMEM, VMEM],
        VMEM,
        (rows, w_rows),
        deps,
        pins={1: pltpu.VMEM},
        flops=PRODUCT,
    )


def round_merged(product, bias, deps=()):
    def kernel(product_ref, bias_ref, out_ref):
        out_ref[...] = (product_ref[...] + bias_ref[...].astype(F32)).astype(BF)

    return call(
        kernel,
        "round_merged",
        pltpu.VMEM(product.shape, BF),
        [VMEM, VMEM],
        VMEM,
        (product, bias),
        deps,
    )


def place_rows(slots, hot, pieces, text, deps=()):
    tokens, width = text.shape
    block = 512
    total = hot.shape[1]
    arrays, parts = zip(*pieces)
    spans = [slice(start, start + block) for start in range(0, width, block)]

    def kernel(slot_ref, hot_ref, text_ref, *refs):
        ins, out_ref, wire_ref, done_ref, sems = refs[:-4], *refs[-4:]
        used = as_column((slot_ref[...] >= 0).astype(I32))
        gather(wire_ref, ins, parts)
        copies = []
        for i, span in enumerate(spans):
            rows = jnp.dot(hot_ref[...], wire_ref[:, span], preferred_element_type=F32)
            done_ref[:, span] = jnp.where(
                used > 0, rows, text_ref[:, span].astype(F32)
            ).astype(BF)
            copies.append(
                pltpu.make_async_copy(done_ref.at[:, span], out_ref.at[:, span], sems.at[i])
            )
            copies[-1].start()
        for copy in copies:
            copy.wait()

    return call(
        kernel,
        "place_rows",
        pltpu.HBM((tokens, width), BF),
        [VMEM] * (3 + len(arrays)),
        ANY,
        (slots, hot, text, *arrays),
        deps,
        limit=12,
        flops=PLACE,
        scratch_shapes=[
            pltpu.VMEM((total, width), BF),
            pltpu.VMEM((tokens, width), BF),
            pltpu.SemaphoreType.DMA((len(spans),)),
        ],
    )


def add_term(own, other, deps=(), weight=1):
    def kernel(a_ref, b_ref, out_ref):
        out_ref[...] = (a_ref[...].astype(F32) + b_ref[...].astype(F32)).astype(BF)

    shape = pltpu.VMEM(own.shape, BF)
    return call(
        kernel, "add_term", shape, [VMEM, VMEM], VMEM, (own, other), deps, limit=4, flops=weight * NODE
    )


def add_and_choose(inner, own, other, term, deps=()):
    def kernel(inner_ref, a_ref, b_ref, term_ref, sum_ref, next_ref):
        total = (a_ref[...].astype(F32) + b_ref[...].astype(F32)).astype(BF)
        sum_ref[...] = total
        next_ref[...] = jnp.where(
            inner_ref[0] > 0, total.astype(F32), term_ref[...].astype(F32)
        ).astype(BF)

    shape = pltpu.VMEM(own.shape, BF)
    return call(
        kernel,
        "add_and_choose",
        (shape, shape),
        [SMEM, VMEM, VMEM, VMEM],
        (VMEM, VMEM),
        (inner, own, other, term),
        deps,
        limit=4,
        flops=NODE,
    )


def finish(inner, hot, sums, slope, so_far, first, width, deps=()):
    n, depth = slope.shape
    flat = [array for pair in sums for array in pair]

    def kernel(inner_ref, hot_ref, slope_ref, *refs):
        ins = refs[: len(flat)]
        out_ref, rows_ref, done_ref, sem = refs[-4:]
        start = 0
        for held, came in zip(ins[::2], ins[1::2]):
            block = jnp.where(
                inner_ref[0] > 0, held[...].astype(F32), came[...].astype(F32)
            ).astype(BF)
            height = held.shape[0]
            for i in range(held.shape[1] // width):
                rows_ref[start : start + height] = block[:, i * width : (i + 1) * width]
                start += height
        total = jnp.dot(hot_ref[...], rows_ref[...], preferred_element_type=F32)
        slopes = slope_ref[:, first : first + width]
        done_ref[...] = (total * slopes.astype(F32)).astype(BF)
        copy = pltpu.make_async_copy(done_ref, out_ref.at[:, first : first + width], sem)
        copy.start()
        copy.wait()

    args = (inner, hot, slope, *flat)
    in_specs = [SMEM] + [VMEM] * (2 + len(flat))
    aliases, pins = {}, {}
    if so_far is not None:
        aliases = {len(args): 0}
        pins = {len(args): pltpu.HBM}
        args += (so_far,)
        in_specs.append(ANY)
    return call(
        kernel,
        "finish",
        pltpu.HBM((n, depth), BF),
        in_specs,
        ANY,
        args,
        deps,
        pins=pins,
        flops=FINISH,
        scratch_shapes=[
            pltpu.VMEM((n, width), BF),
            pltpu.VMEM((n, width), BF),
            pltpu.SemaphoreType.DMA,
        ],
        input_output_aliases=aliases,
    )


def pipelined(pre_act, w_out, b_out, row_slot, ctx_slot, text_rows, cotangent):
    ctx_size, grp_size, tp_size = (lax.axis_size(name) for name in ("ctx", "grp", "tp"))
    groups = ctx_size * grp_size
    rows, depth = pre_act.shape
    width = w_out.shape[1]
    tokens = ctx_slot.shape[0]
    capacity = 2 * rows // groups
    shift = capacity.bit_length() - 1
    me = (lax.axis_index("ctx") * grp_size + lax.axis_index("grp")).reshape(1)
    tp_index = lax.axis_index("tp")
    inner = ((tp_index == 1) | (tp_index == 2)).astype(I32).reshape(1)
    row_slots = row_slot.reshape(1, rows)
    ctx_slots = ctx_slot.reshape(1, tokens)

    pair = grp_size

    def exchange(k, piece):
        return lax.ppermute(piece, GROUP_AXES, [(i, i ^ k) for i in range(groups)])

    def whole(array):
        return array, slice(0, array.shape[0])

    def exchange_pair(i, sent):
        return exchange((i // pair) * 2 * pair + i % pair, sent)

    def exchange_pairs(sent):
        return [sent[0]] + [exchange_pair(i, sent[i]) for i in range(1, len(sent))]

    def relayed(came, deps=()):
        half = came[0].shape[0] // 2
        last = exchange(pair, relay(came, deps))
        return [(array, slice(0, half)) for array in came] + [whole(last)]

    early = capacity // 2
    late = capacity - early
    early_rows = rows // 2
    per_part = 5
    size = depth // per_part
    chunks = 2 * per_part
    half = groups // 2

    bias = b_out.reshape(1, width)
    first_out, held = pack_context(
        me, inner, ctx_slots, cotangent, 0, early, shift, groups, pair
    )
    first_in = exchange_pairs(first_out)
    (
        hot_early, hot_all, hot_back, hot_late, hot_merged, hot_place,
        w_here, forward, slope,
    ) = prepare(
        me, row_slots, ctx_slots, early, shift, groups, pair, pre_act, w_out, (first_out[1],)
    )

    def exchange_in_turn(hot, sent, height, deps):
        stay, swaps = split_rows(hot, sent, half, deps)
        got = [exchange(pair, swap) for swap in swaps]
        came = [(stay, slice(0, height)), whole(got[0])]
        offsets = [(i // pair) * 2 * pair + i % pair for i in range(1, half)]
        blocks = {}
        for straight in (True, False):
            after = tuple(blocks.values())
            for i, offset in enumerate(offsets, 1):
                if (offset & (offset - 1) == 0) == straight:
                    blocks[i] = exchange(offset, join(stay, got[i], i, height, after))
        return came + [whole(blocks[i]) for i in range(1, half)]

    def product(j, deps=()):
        span = slice(0, early_rows) if j < per_part else slice(early_rows, rows)
        first = j % per_part * size
        return back_product(grads, w_here, span, first, first + size, deps)

    first_in = relayed(first_in, (forward,))
    grads = take_rows(hot_early, first_in)
    terms = {0: product(0)}
    terms[1] = product(1, (terms[0],))
    second_in = exchange_in_turn(hot_late, held, late, (terms[1],))
    outer_pairs = [(0, 1), (1, 0), (2, 3), (3, 2)]
    inner_pairs = [
        (c * tp_size + t, c * tp_size + 3 - t if t in (1, 2) else (c ^ 1) * tp_size + t)
        for c in range(ctx_size)
        for t in range(tp_size)
    ]
    from_pair, from_far, halves, totals, send = {}, {}, {}, {}, {}

    def to_pair(j, value):
        from_pair[j] = lax.ppermute(value, "tp", outer_pairs)

    def finish_block(k, so_far, *deps):
        sums = [(totals[i], from_pair[i + 3]) for i in (k, k + per_part)]
        return finish(inner, hot_back, sums, slope, so_far, k * size, size, deps)

    to_pair(0, terms[0])
    to_pair(1, terms[1])
    grad_pre = None
    for j in range(chunks):
        after = []
        ahead = j + 2
        if ahead < chunks:
            previous = (send[j + 1],) if j >= 2 else (terms[j + 1],)
            if ahead == per_part:
                grads = take_rows(hot_all, first_in + second_in, previous)
            terms[ahead] = product(ahead, previous)
            if ahead != per_part:
                after.append(terms[ahead])
        if j == 4:
            merged = round_merged(forward, bias, (halves[j - 1],))
            arrived = exchange_in_turn(hot_merged, merged, capacity, (halves[j - 1],))
        if j == chunks - 1:
            grad_pre = finish_block(0, None, halves[j - 1])
            after.append(grad_pre)
        halves[j] = add_term(terms[j], from_pair[j], tuple(after))
        from_far[j] = lax.ppermute(halves[j], ("ctx", "tp"), inner_pairs)
        if j == 0:
            value, _ = lax.optimization_barrier((terms[2], halves[0]))
            to_pair(2, value)
        elif ahead < chunks:
            totals[j - 1], send[ahead] = add_and_choose(
                inner, halves[j - 1], from_far[j - 1], terms[ahead], (halves[j],)
            )
            to_pair(ahead, send[ahead])
        else:
            totals[j - 1] = add_term(halves[j - 1], from_far[j - 1], (halves[j],))
            to_pair(ahead, totals[j - 1])
    grad_pre = finish_block(1, grad_pre, totals[chunks - 2])
    totals[chunks - 1] = add_term(halves[chunks - 1], from_far[chunks - 1], (grad_pre,))
    to_pair(chunks + 2, totals[chunks - 1])
    embeds = place_rows(ctx_slots, hot_place, arrived, text_rows, (halves[chunks - 2],))
    for k in range(2, per_part):
        grad_pre = finish_block(k, grad_pre, *([embeds] if k == 3 else []))
    return embeds, grad_pre


def shards(pre_act, w_out, b_out, row_slot, ctx_slot, text_rows, cotangent):
    groups = lax.axis_size("ctx") * lax.axis_size("grp")
    rows, depth = pre_act.shape
    width = w_out.shape[1]
    capacity = 2 * rows // groups
    power = lambda value: value & (value - 1) == 0
    fits = (
        lax.axis_size("tp") == 4
        and lax.axis_size("ctx") % 2 == 0
        and 4 <= groups <= 8
        and power(groups)
        and power(capacity)
        and capacity % 32 == 0
        and rows % 256 == 0
        and ctx_slot.shape[0] % 128 == 0
        and depth % 5120 == 0
        and width % 512 == 0
    )
    plan = pipelined if fits else plain
    return plan(pre_act, w_out, b_out, row_slot, ctx_slot, text_rows, cotangent)


def solution(mesh):
    in_specs = (
        P(("ctx", "grp"), None),
        P(None, "tp"),
        P("tp"),
        P(("ctx", "grp")),
        P(("ctx", "grp")),
        P(("ctx", "grp"), "tp"),
        P(("ctx", "grp"), "tp"),
    )
    out_specs = (P(("ctx", "grp"), "tp"), P(("ctx", "grp"), None))
    return jax.shard_map(shards, mesh=mesh, in_specs=in_specs, out_specs=out_specs, check_vma=False)
```

```python
import functools
import math

import jax
import jax.numpy as jnp
from jax import lax
from jax.experimental import pallas as pl
from jax.experimental.pallas import tpu as pltpu
from jax.sharding import PartitionSpec as P

BF = jnp.bfloat16
F32 = jnp.float32
I32 = jnp.int32
GROUP_AXES = ("ctx", "grp")
VMEM = pl.BlockSpec(memory_space=pltpu.VMEM)
SMEM = pl.BlockSpec(memory_space=pltpu.SMEM)
ANY = pl.BlockSpec(memory_space=pl.ANY)
NODE = 800_000_000
TAKE = 3_200_000_000
PLACE = 6_400_000_000
FINISH = 1_000_000_000
PRODUCT = 400_000_000


def gelu_value(values):
    return 0.5 * values * (1.0 + lax.erf(values * 0.7071067811865476))


def gelu_slope(values):
    return (
        0.5 * (1.0 + lax.erf(values * 0.7071067811865476))
        + values * jnp.exp(-0.5 * values * values) * 0.3989422804014327
    )


def plain(pre_act, w_out, b_out, row_slot, ctx_slot, text_rows, cotangent):
    groups = lax.axis_size("ctx") * lax.axis_size("grp")
    slot_count = 2 * pre_act.shape[0]
    capacity = slot_count // groups
    width = w_out.shape[1]
    pre_float = pre_act.astype(F32)
    hidden = gelu_value(pre_float).astype(BF)
    merged = (jnp.dot(hidden, w_out, preferred_element_type=F32) + b_out.astype(F32)).astype(BF)
    outgoing = jnp.zeros((slot_count, width), BF).at[row_slot].set(merged)
    placed = ctx_slot >= 0
    returning = (
        jnp.zeros((slot_count, width), BF)
        .at[jnp.where(placed, ctx_slot, slot_count)]
        .set(cotangent, mode="drop")
    )

    def exchange(sent):
        blocks = sent.reshape(groups, capacity, width)
        return lax.all_to_all(
            blocks, GROUP_AXES, split_axis=0, concat_axis=0, tiled=True
        ).reshape(slot_count, width)

    arrived = exchange(outgoing)
    embeds = jnp.where(placed[:, None], arrived[jnp.where(placed, ctx_slot, 0)], text_rows)
    grad_rows = exchange(returning)[row_slot]
    partial_value = lax.dot_general(
        grad_rows, w_out, (((1,), (1,)), ((), ())), preferred_element_type=F32
    )
    summed = lax.psum(partial_value.astype(BF), "tp").astype(F32)
    grad_pre = (summed * gelu_slope(pre_float)).astype(BF)
    return embeds, grad_pre


def iota(shape, axis):
    return lax.broadcasted_iota(I32, shape, axis)


def as_column(row):
    n = row.shape[1]
    return jnp.sum(jnp.where(iota((n, n), 0) == iota((n, n), 1), row, 0), axis=1, keepdims=True)


def rank_in_block(row, shift):
    column = as_column(row)
    smaller = ((column >> shift) == (row >> shift)) & (column < row) & (column >= 0)
    return jnp.sum(smaller.astype(I32), axis=0, keepdims=True)


def arrival(row, shift, early):
    n = row.shape[1]
    rank = rank_in_block(row, shift)
    is_early = (rank < early).astype(I32)
    before = jnp.sum(
        jnp.where(iota((n, n), 0) < iota((n, n), 1), as_column(is_early), 0), axis=0, keepdims=True
    )
    index = iota((1, n), 1)
    place = jnp.where(is_early > 0, before, jnp.sum(is_early) + index - before)
    return rank, is_early, place


def call(kernel, name, out_shape, in_specs, out_specs, args, deps=(), limit=8, pins=None, flops=1000, **more):
    n = len(args)
    pins = pins or {}
    args = [
        pltpu.with_memory_space_constraint(arg, pins[i]) if i in pins else arg
        for i, arg in enumerate(args)
    ]
    deps = [
        pltpu.with_memory_space_constraint(dep, pltpu.HBM) if dep.size >= 1 << 20 else dep
        for dep in deps
    ]

    def body(*refs):
        kernel(*refs[:n], *refs[n + len(deps) :])

    return pl.pallas_call(
        body,
        out_shape=out_shape,
        in_specs=list(in_specs) + [ANY] * len(deps),
        out_specs=out_specs,
        cost_estimate=pl.CostEstimate(flops=flops, bytes_accessed=flops // 300, transcendentals=0),
        compiler_params=pltpu.CompilerParams(vmem_limit_bytes=limit << 20),
        name=name,
        **more,
    )(*args, *deps)


def full(shape):
    return pl.BlockSpec(shape, lambda *_: (0,) * len(shape))


def columns(rows, block):
    return pl.BlockSpec((rows, block), lambda i: (0, i))


def as_hot(mask):
    return jnp.where(mask, 1.0, 0.0).astype(BF)


def place_of(offset, pair):
    return ((offset & ~(2 * pair - 1)) >> 1) | (offset & (pair - 1))


def goes_to(offset, pair):
    return place_of(offset, pair) * 2 + jnp.where((offset & pair) > 0, 1, 0)


def came_from(offset, pair, groups):
    return place_of(offset, pair) + jnp.where((offset & pair) > 0, groups // 2, 0)


def pack_context(me, inner, slots, cotangent, low, high, shift, groups, pair):
    tokens, width = cotangent.shape
    count = high - low
    spans = [slice(start, start + 512) for start in range(0, width, 512)]
    parts = groups // 2
    height = 2 * count

    def kernel(me_ref, inner_ref, slot_ref, rows_ref, *refs):
        outs, held_ref, here_ref, sems = refs[:parts], *refs[parts:]
        slots_copy = pltpu.make_async_copy(slot_ref, here_ref, sems.at[0])
        copy = pltpu.make_async_copy(rows_ref, held_ref, sems.at[1])
        slots_copy.start()
        copy.start()
        slots_copy.wait()
        row = here_ref[...]
        rank = rank_in_block(row, shift)
        used = (row >= 0) & (rank >= low) & (rank < high)
        wire = goes_to((row >> shift) ^ me_ref[0], pair) * count + rank - low
        hot = as_hot(iota((groups * count, tokens), 0) == jnp.where(used, wire, -1))
        copy.wait()
        for span in spans:
            packed = jnp.dot(hot, held_ref[:, span], preferred_element_type=F32).astype(BF)
            for k, out in enumerate(outs):
                out[:, span] = packed[k * height : (k + 1) * height]

    *outs, held = call(
        kernel,
        "pack_context",
        [pltpu.VMEM((height, width), BF)] * parts + [pltpu.VMEM((tokens, width), BF)],
        [SMEM, SMEM, ANY, ANY],
        [VMEM] * (parts + 1),
        (me, inner, slots, cotangent),
        pins={2: pltpu.HBM, 3: pltpu.HBM},
        scratch_shapes=[pltpu.VMEM((1, tokens), I32), pltpu.SemaphoreType.DMA((2,))],
    )
    return outs, held


def split_rows(hot, rows, parts, deps=()):
    half, width = hot.shape[0] // 2, rows.shape[1]
    height = half // parts

    def kernel(hot_ref, rows_ref, stay_ref, *swap_refs):
        for start in range(0, width, 512):
            span = slice(start, start + 512)
            packed = jnp.dot(hot_ref[...], rows_ref[:, span], preferred_element_type=F32)
            packed = packed.astype(BF)
            stay_ref[:, span] = packed[:half]
            for i, swap_ref in enumerate(swap_refs):
                first = half + i * height
                swap_ref[:, span] = packed[first : first + height]

    stay, *swaps = call(
        kernel,
        "split_rows",
        [pltpu.VMEM((half, width), BF)] + [pltpu.VMEM((height, width), BF)] * parts,
        [VMEM, VMEM],
        [VMEM] * (1 + parts),
        (hot, rows),
        deps,
    )
    return stay, swaps


def join(stay, got, index, height, deps=()):
    span = slice(index * height, (index + 1) * height)

    def kernel(stay_ref, got_ref, out_ref):
        out_ref[:height] = stay_ref[span]
        out_ref[height:] = got_ref[...]

    return call(
        kernel,
        "join",
        pltpu.VMEM((2 * height, stay.shape[1]), BF),
        [VMEM, VMEM],
        VMEM,
        (stay, got),
        deps,
    )


def relay(pieces, deps=()):
    height, width = pieces[0].shape
    half = height // 2

    def kernel(*refs):
        for i, piece in enumerate(refs[:-1]):
            refs[-1][i * half : (i + 1) * half] = piece[half:]

    return call(
        kernel,
        "relay",
        pltpu.VMEM((len(pieces) * half, width), BF),
        [VMEM] * len(pieces),
        VMEM,
        pieces,
        deps,
    )


def prepare(me, row_slots, ctx_slots, early, shift, groups, pair, pre_act, w_out, deps=()):
    n, depth = pre_act.shape
    width = w_out.shape[1]
    tokens = ctx_slots.shape[1]
    capacity = 1 << shift
    late = capacity - early
    half = n * early // capacity
    wires = groups * capacity
    spans = [slice(start, start + 512) for start in range(0, depth, 512)]

    def kernel(me_ref, row_hbm, ctx_hbm, pre_hbm, w_hbm, *refs):
        early_ref, all_ref, back_ref, late_ref, merged_ref, place_ref = refs[:6]
        w_ref, product_ref, slope_hbm = refs[6:9]
        row_ref, ctx_ref, pre_ref, slope_ref, sems = refs[9:]
        small = [
            pltpu.make_async_copy(row_hbm, row_ref, sems.at[len(spans)]),
            pltpu.make_async_copy(ctx_hbm, ctx_ref, sems.at[len(spans) + 1]),
        ]
        values_copy = pltpu.make_async_copy(pre_hbm, pre_ref, sems.at[len(spans) + 2])
        copies = [
            pltpu.make_async_copy(w_hbm.at[span], w_ref.at[span], sems.at[i])
            for i, span in enumerate(spans)
        ]
        for copy in [*small, values_copy, *copies]:
            copy.start()
        for copy in small:
            copy.wait()
        row = row_ref[...]
        offset = (row >> shift) ^ me_ref[0]
        rank, is_early, place = arrival(row, shift, early)
        wire = jnp.where(
            is_early > 0,
            came_from(offset, pair, groups) * early + rank,
            groups * early + goes_to(offset, pair) * late + rank - early,
        )
        order = iota((n, n), 0) == place
        source = jnp.sum(jnp.where(order, wire, 0), axis=1, keepdims=True)
        early_ref[...] = as_hot(iota((half, groups * early), 1) == source[:half])
        all_ref[...] = as_hot(iota((n, wires), 1) == source)
        back_ref[...] = as_hot(iota((n, n), 1) == as_column(place))
        target = (came_from(offset, pair, groups) << shift) + (row & (capacity - 1))
        merged_ref[...] = as_hot(iota((wires, n), 0) == target)
        ctx = ctx_ref[...]
        offset = (ctx >> shift) ^ me_ref[0]
        rank = rank_in_block(ctx, shift)
        target = came_from(offset, pair, groups) * late + rank - early
        target = jnp.where((ctx >= 0) & (rank >= early), target, -1)
        late_ref[...] = as_hot(iota((groups * late, tokens), 0) == target)
        source = (goes_to(offset, pair) << shift) + (ctx & (capacity - 1))
        source = as_column(jnp.where(ctx >= 0, source, -1))
        place_ref[...] = as_hot(iota((tokens, wires), 1) == source)
        values_copy.wait()
        slope_copies = []
        for i, (copy, span) in enumerate(zip(copies, spans)):
            values = pre_ref[:, span].astype(F32)
            share = 0.5 * (1.0 + lax.erf(values * 0.7071067811865476))
            slope = share + values * jnp.exp(-0.5 * values * values) * 0.3989422804014327
            slope_ref[:, span] = slope.astype(BF)
            slope_copies.append(
                pltpu.make_async_copy(
                    slope_ref.at[:, span], slope_hbm.at[:, span], sems.at[len(spans) + 3 + i]
                )
            )
            slope_copies[-1].start()
            copy.wait()
            term = jnp.dot(
                (values * share).astype(BF), w_ref[span], preferred_element_type=F32
            )
            if i == 0:
                product_ref[...] = term
            else:
                product_ref[...] += term
        for copy in slope_copies:
            copy.wait()

    shapes = [
        (half, groups * early),
        (n, wires),
        (n, n),
        (groups * late, tokens),
        (wires, n),
        (tokens, wires),
        (depth, width),
    ]
    return call(
        kernel,
        "prepare",
        [pltpu.VMEM(shape, BF) for shape in shapes]
        + [pltpu.VMEM((n, width), F32), pltpu.HBM((n, depth), BF)],
        [SMEM] + [ANY] * 4,
        [VMEM] * 8 + [ANY],
        (me, row_slots, ctx_slots, pre_act, w_out),
        deps,
        limit=10,
        pins={i: pltpu.HBM for i in range(1, 5)},
        flops=4 * n * depth * width,
        scratch_shapes=[
            pltpu.VMEM((1, n), I32),
            pltpu.VMEM((1, tokens), I32),
            pltpu.VMEM((n, depth), BF),
            pltpu.VMEM((n, depth), BF),
            pltpu.SemaphoreType.DMA((2 * len(spans) + 3,)),
        ],
    )


def dot_columns(hot, rows_ref, out_ref, block=512):
    for start in range(0, out_ref.shape[1], block):
        span = slice(start, start + block)
        out_ref[:, span] = jnp.dot(
            hot, rows_ref[:, span], preferred_element_type=F32
        ).astype(BF)


def gather(wire_ref, refs, spans):
    start = 0
    for ref, span in zip(refs, spans):
        height = span.stop - span.start
        wire_ref[start : start + height] = ref[span]
        start += height


def take_rows(hot, pieces, deps=()):
    arrays, spans = zip(*pieces)
    width = arrays[0].shape[1]

    def kernel(hot_ref, *refs):
        ins, out_ref, wire_ref = refs[:-2], refs[-2], refs[-1]
        gather(wire_ref, ins, spans)
        dot_columns(hot_ref[...], wire_ref, out_ref)

    return call(
        kernel,
        "take_rows",
        pltpu.VMEM((hot.shape[0], width), BF),
        [VMEM] * (1 + len(arrays)),
        VMEM,
        (hot, *arrays),
        deps,
        flops=TAKE,
        scratch_shapes=[pltpu.VMEM((hot.shape[1], width), BF)],
    )


def back_product(rows, w_rows, span, first, last, deps=()):
    def kernel(rows_ref, w_ref, out_ref):
        out_ref[...] = lax.dot_general(
            rows_ref[span],
            w_ref[first:last],
            (((1,), (1,)), ((), ())),
            preferred_element_type=F32,
        ).astype(BF)

    return call(
        kernel,
        "back_product",
        pltpu.VMEM((span.stop - span.start, last - first), BF),
        [VMEM, VMEM],
        VMEM,
        (rows, w_rows),
        deps,
        pins={1: pltpu.VMEM},
        flops=PRODUCT,
    )


def round_merged(product, bias, deps=()):
    def kernel(product_ref, bias_ref, out_ref):
        out_ref[...] = (product_ref[...] + bias_ref[...].astype(F32)).astype(BF)

    return call(
        kernel,
        "round_merged",
        pltpu.VMEM(product.shape, BF),
        [VMEM, VMEM],
        VMEM,
        (product, bias),
        deps,
    )


def place_rows(slots, hot, pieces, text, deps=()):
    tokens, width = text.shape
    block = 512
    total = hot.shape[1]
    arrays, parts = zip(*pieces)
    spans = [slice(start, start + block) for start in range(0, width, block)]

    def kernel(slot_ref, hot_ref, text_ref, *refs):
        ins, out_ref, wire_ref, done_ref, sems = refs[:-4], *refs[-4:]
        used = as_column((slot_ref[...] >= 0).astype(I32))
        gather(wire_ref, ins, parts)
        copies = []
        for i, span in enumerate(spans):
            rows = jnp.dot(hot_ref[...], wire_ref[:, span], preferred_element_type=F32)
            done_ref[:, span] = jnp.where(
                used > 0, rows, text_ref[:, span].astype(F32)
            ).astype(BF)
            copies.append(
                pltpu.make_async_copy(done_ref.at[:, span], out_ref.at[:, span], sems.at[i])
            )
            copies[-1].start()
        for copy in copies:
            copy.wait()

    return call(
        kernel,
        "place_rows",
        pltpu.HBM((tokens, width), BF),
        [VMEM] * (3 + len(arrays)),
        ANY,
        (slots, hot, text, *arrays),
        deps,
        limit=12,
        flops=PLACE,
        scratch_shapes=[
            pltpu.VMEM((total, width), BF),
            pltpu.VMEM((tokens, width), BF),
            pltpu.SemaphoreType.DMA((len(spans),)),
        ],
    )


def add_term(own, other, deps=(), weight=1):
    def kernel(a_ref, b_ref, out_ref):
        out_ref[...] = (a_ref[...].astype(F32) + b_ref[...].astype(F32)).astype(BF)

    shape = pltpu.VMEM(own.shape, BF)
    return call(
        kernel, "add_term", shape, [VMEM, VMEM], VMEM, (own, other), deps, limit=4, flops=weight * NODE
    )


def add_and_choose(inner, own, other, term, deps=()):
    def kernel(inner_ref, a_ref, b_ref, term_ref, sum_ref, next_ref):
        total = (a_ref[...].astype(F32) + b_ref[...].astype(F32)).astype(BF)
        sum_ref[...] = total
        next_ref[...] = jnp.where(
            inner_ref[0] > 0, total.astype(F32), term_ref[...].astype(F32)
        ).astype(BF)

    shape = pltpu.VMEM(own.shape, BF)
    return call(
        kernel,
        "add_and_choose",
        (shape, shape),
        [SMEM, VMEM, VMEM, VMEM],
        (VMEM, VMEM),
        (inner, own, other, term),
        deps,
        limit=4,
        flops=NODE,
    )


def finish(inner, hot, sums, slope, so_far, first, width, deps=()):
    n, depth = slope.shape
    flat = [array for pair in sums for array in pair]

    def kernel(inner_ref, hot_ref, slope_ref, *refs):
        ins = refs[: len(flat)]
        out_ref, rows_ref, done_ref, sem = refs[-4:]
        start = 0
        for held, came in zip(ins[::2], ins[1::2]):
            block = jnp.where(
                inner_ref[0] > 0, held[...].astype(F32), came[...].astype(F32)
            ).astype(BF)
            height = held.shape[0]
            for i in range(held.shape[1] // width):
                rows_ref[start : start + height] = block[:, i * width : (i + 1) * width]
                start += height
        total = jnp.dot(hot_ref[...], rows_ref[...], preferred_element_type=F32)
        slopes = slope_ref[:, first : first + width]
        done_ref[...] = (total * slopes.astype(F32)).astype(BF)
        copy = pltpu.make_async_copy(done_ref, out_ref.at[:, first : first + width], sem)
        copy.start()
        copy.wait()

    args = (inner, hot, slope, *flat)
    in_specs = [SMEM] + [VMEM] * (2 + len(flat))
    aliases, pins = {}, {}
    if so_far is not None:
        aliases = {len(args): 0}
        pins = {len(args): pltpu.HBM}
        args += (so_far,)
        in_specs.append(ANY)
    return call(
        kernel,
        "finish",
        pltpu.HBM((n, depth), BF),
        in_specs,
        ANY,
        args,
        deps,
        pins=pins,
        flops=FINISH,
        scratch_shapes=[
            pltpu.VMEM((n, width), BF),
            pltpu.VMEM((n, width), BF),
            pltpu.SemaphoreType.DMA,
        ],
        input_output_aliases=aliases,
    )


def pipelined(pre_act, w_out, b_out, row_slot, ctx_slot, text_rows, cotangent):
    ctx_size, grp_size, tp_size = (lax.axis_size(name) for name in ("ctx", "grp", "tp"))
    groups = ctx_size * grp_size
    rows, depth = pre_act.shape
    width = w_out.shape[1]
    tokens = ctx_slot.shape[0]
    capacity = 2 * rows // groups
    shift = capacity.bit_length() - 1
    me = (lax.axis_index("ctx") * grp_size + lax.axis_index("grp")).reshape(1)
    tp_index = lax.axis_index("tp")
    inner = ((tp_index == 1) | (tp_index == 2)).astype(I32).reshape(1)
    row_slots = row_slot.reshape(1, rows)
    ctx_slots = ctx_slot.reshape(1, tokens)

    pair = grp_size

    def exchange(k, piece):
        return lax.ppermute(piece, GROUP_AXES, [(i, i ^ k) for i in range(groups)])

    def whole(array):
        return array, slice(0, array.shape[0])

    def exchange_pair(i, sent):
        return exchange((i // pair) * 2 * pair + i % pair, sent)

    def exchange_pairs(sent):
        return [sent[0]] + [exchange_pair(i, sent[i]) for i in range(1, len(sent))]

    def relayed(came, deps=()):
        half = came[0].shape[0] // 2
        last = exchange(pair, relay(came, deps))
        return [(array, slice(0, half)) for array in came] + [whole(last)]

    early = capacity // 2
    late = capacity - early
    early_rows = rows // 2
    per_part = 5
    size = depth // per_part
    chunks = 2 * per_part
    half = groups // 2

    bias = b_out.reshape(1, width)
    first_out, held = pack_context(
        me, inner, ctx_slots, cotangent, 0, early, shift, groups, pair
    )
    first_in = exchange_pairs(first_out)
    (
        hot_early, hot_all, hot_back, hot_late, hot_merged, hot_place,
        w_here, forward, slope,
    ) = prepare(
        me, row_slots, ctx_slots, early, shift, groups, pair, pre_act, w_out, (first_out[1],)
    )

    def exchange_in_turn(hot, sent, height, deps):
        stay, swaps = split_rows(hot, sent, half, deps)
        got = [exchange(pair, swap) for swap in swaps]
        came = [(stay, slice(0, height)), whole(got[0])]
        offsets = [(i // pair) * 2 * pair + i % pair for i in range(1, half)]
        blocks = {}
        for straight in (True, False):
            after = tuple(blocks.values())
            for i, offset in enumerate(offsets, 1):
                if (offset & (offset - 1) == 0) == straight:
                    blocks[i] = exchange(offset, join(stay, got[i], i, height, after))
        return came + [whole(blocks[i]) for i in range(1, half)]

    def product(j, deps=()):
        span = slice(0, early_rows) if j < per_part else slice(early_rows, rows)
        first = j % per_part * size
        return back_product(grads, w_here, span, first, first + size, deps)

    first_in = relayed(first_in, (forward,))
    grads = take_rows(hot_early, first_in)
    terms = {0: product(0)}
    terms[1] = product(1, (terms[0],))
    second_in = exchange_in_turn(hot_late, held, late, (terms[1],))
    outer_pairs = [(0, 1), (1, 0), (2, 3), (3, 2)]
    inner_pairs = [
        (c * tp_size + t, c * tp_size + 3 - t if t in (1, 2) else (c ^ 1) * tp_size + t)
        for c in range(ctx_size)
        for t in range(tp_size)
    ]
    from_pair, from_far, halves, totals, send = {}, {}, {}, {}, {}

    def to_pair(j, value):
        from_pair[j] = lax.ppermute(value, "tp", outer_pairs)

    def finish_block(k, so_far, *deps):
        sums = [(totals[i], from_pair[i + 3]) for i in (k, k + per_part)]
        return finish(inner, hot_back, sums, slope, so_far, k * size, size, deps)

    to_pair(0, terms[0])
    to_pair(1, terms[1])
    grad_pre = None
    for j in range(chunks):
        after = []
        ahead = j + 2
        if ahead < chunks:
            previous = (send[j + 1],) if j >= 2 else (terms[j + 1],)
            if ahead == per_part:
                grads = take_rows(hot_all, first_in + second_in, previous)
            terms[ahead] = product(ahead, previous)
            if ahead != per_part:
                after.append(terms[ahead])
        if j == 4:
            merged = round_merged(forward, bias, (halves[j - 1],))
            arrived = exchange_in_turn(hot_merged, merged, capacity, (halves[j - 1],))
        if j == chunks - 1:
            grad_pre = finish_block(0, None, halves[j - 1])
            after.append(grad_pre)
        halves[j] = add_term(terms[j], from_pair[j], tuple(after))
        from_far[j] = lax.ppermute(halves[j], ("ctx", "tp"), inner_pairs)
        if j == 0:
            value, _ = lax.optimization_barrier((terms[2], halves[0]))
            to_pair(2, value)
        elif ahead < chunks:
            totals[j - 1], send[ahead] = add_and_choose(
                inner, halves[j - 1], from_far[j - 1], terms[ahead], (halves[j],)
            )
            to_pair(ahead, send[ahead])
        else:
            weight = {chunks - 2: 4, chunks - 1: 2}.get(j, 1)
            totals[j - 1] = add_term(halves[j - 1], from_far[j - 1], (halves[j],), weight)
            to_pair(ahead, totals[j - 1])
    grad_pre = finish_block(1, grad_pre, totals[chunks - 2])
    totals[chunks - 1] = add_term(halves[chunks - 1], from_far[chunks - 1], (grad_pre,))
    to_pair(chunks + 2, totals[chunks - 1])
    embeds = place_rows(ctx_slots, hot_place, arrived, text_rows, (halves[chunks - 2],))
    for k in range(2, per_part):
        grad_pre = finish_block(k, grad_pre, *([embeds] if k == 3 else []))
    return embeds, grad_pre


def shards(pre_act, w_out, b_out, row_slot, ctx_slot, text_rows, cotangent):
    groups = lax.axis_size("ctx") * lax.axis_size("grp")
    rows, depth = pre_act.shape
    width = w_out.shape[1]
    capacity = 2 * rows // groups
    power = lambda value: value & (value - 1) == 0
    fits = (
        lax.axis_size("tp") == 4
        and lax.axis_size("ctx") % 2 == 0
        and 4 <= groups <= 8
        and power(groups)
        and power(capacity)
        and capacity % 32 == 0
        and rows % 256 == 0
        and ctx_slot.shape[0] % 128 == 0
        and depth % 5120 == 0
        and width % 512 == 0
    )
    plan = pipelined if fits else plain
    return plan(pre_act, w_out, b_out, row_slot, ctx_slot, text_rows, cotangent)


def solution(mesh):
    in_specs = (
        P(("ctx", "grp"), None),
        P(None, "tp"),
        P("tp"),
        P(("ctx", "grp")),
        P(("ctx", "grp")),
        P(("ctx", "grp"), "tp"),
        P(("ctx", "grp"), "tp"),
    )
    out_specs = (P(("ctx", "grp"), "tp"), P(("ctx", "grp"), None))
    return jax.shard_map(shards, mesh=mesh, in_specs=in_specs, out_specs=out_specs, check_vma=False)
```
